128 devices in a mesh: group: 4 (over x), dev: 32 (over y, z, core).
Axes of the slice: x: 4, y: 4, z: 4, core: 2. Of those that a mesh axis runs over, the one named last changes fastest.
Arguments:
- density: float32 [128, 320, 128], P(('group', 'dev')), may hold values from 0.5 to 2
- velocity: float32 [3, 128, 320, 128], P(None, ('group', 'dev')), may hold values from -0.75 to 0.75
- pressure: float32 [128, 320, 128], P(('group', 'dev')), may hold values from 0.5 to 2
- rbf_blocks: bfloat16 [8192, 128, 128], P(('group', 'dev')), may hold values from -0.5 to 0.5
- correlation: int32 [8192, 128], P(('group', 'dev')), may hold values from 0 to 319
- normals: float32 [8192, 3, 128], P(('group', 'dev')), may hold values from -6 to 6
- routes: int32 [8192, 1], P(('group', 'dev')), may hold values from 0 to 127; in each aligned block of 64 rows (0 to 63, 64 to 127, ...) at most 2 rows name the same one
- targets: int32 [8192], P(('group', 'dev')), may hold values from 0 to 31
- stiffness: bfloat16 [4096, 128, 128], P(('group', 'dev')), may hold values from -0.35 to 2.35
- coupling: bfloat16 [4096, 128, 128], P(('group', 'dev')), may hold values from -0.5 to 0.5
- inverse_diag: float32 [4096, 3, 128], P(('group', 'dev')), may hold values from 0.5 to 1.5
- displacement: float32 [4096, 3, 128], P(('group', 'dev')), may hold values from -6 to 6
- diff_res: float32 [8, 4096, 3, 128], P(None, ('group', 'dev')), may hold values from -2 to 2
- diff_disp: float32 [8, 4096, 3, 128], P(None, ('group', 'dev')), may hold values from -2.4 to 2.4
Outputs:
- fluid_next: float32 [5, 128, 320, 128], P(None, ('group', 'dev'))
- disp_next: float32 [4096, 3, 128], P(('group', 'dev'))
- wall_motion: float32 [8192, 3, 128], P(('group', 'dev'))
The draws below stay inside these ranges and needn't reach their ends.
Inputs may be any that keep to these rules, and one draw needn't show every extreme that they name: `routes`: among the 64 blocks of one device at most 2 name the same owner, and some device names one owner exactly 2 times.
All inputs are finite; a program needn't handle non-finite values.
Results may differ from the reference program's by a relative error of at most 0.0004.
The reference program's roundings to bfloat16 on the way (of `weighted` and `disp_half`) count: a program that leaves them out, or rounds other values in their place, can miss the bound.
Values may be sent and summed in bfloat16 or wider, within the bound.
No kernel may reach another device: no remote copies, remote signals or barrier semaphores. Data moves between devices by JAX's collectives and lax.ppermute only.
A program may use at most 64 MiB of HBM per device.

```python
import math
import jax
import jax.numpy as jnp
import numpy as np
from jax import lax

CX = 1
CY = 320
CZ = 128
NB = 64
NS = 32
NODES = 128
M = 8
CAP = 2
NX = 128
NBT = 8192
NST = 4096
DEVICES = 128


def newton_parts(key):
    subkeys = jax.random.split(jax.random.fold_in(key, 4099), 7)
    position = (jnp.arange(NST, dtype=jnp.float32) / NST)[None, :, None, None]
    extent = (M, NST, 3, NODES)
    spread = 0.15 * jnp.power(3.0, position)
    private = jnp.clip(jax.random.normal(subkeys[0], extent, jnp.float32), -4.0, 4.0)
    shared = jnp.clip(jax.random.normal(subkeys[1], (1, NST, 3, NODES), jnp.float32), -4.0, 4.0)
    columns = spread * (private + 0.5 * shared)
    resting = 0.5 * jnp.clip(jax.random.normal(subkeys[2], (NST, 3, NODES), jnp.float32), -4.0, 4.0)
    columns = jnp.clip(columns, -2.0, 2.0)
    lead_signs = jnp.where(jax.random.bernoulli(subkeys[3], 0.5, (M,)), 1.0, -1.0)
    growth_signs = jnp.where(jax.random.bernoulli(subkeys[4], 0.5, (M,)), 1.0, -1.0)
    leading = lead_signs * jax.random.uniform(subkeys[5], (M,), jnp.float32, 0.3, 0.8)
    growth = growth_signs * jax.random.uniform(subkeys[6], (M,), jnp.float32, 0.4, 0.8)
    weights = leading[:, None, None, None] + growth[:, None, None, None] * position
    settled = jnp.clip(resting + jnp.sum(weights * columns, axis=0), -6.0, 6.0)
    return (columns, settled)


def draw_diff_res(key, part):
    return newton_parts(key)[0]


def draw_displacement(key, part):
    return newton_parts(key)[1]


def draw_stiffness(key, part):
    noise_key = jax.random.fold_in(key, 8191)
    offdiag = jnp.clip(jax.random.normal(noise_key, (NST, NODES, NODES), jnp.float32) / math.sqrt(NODES), -0.35, 0.35)
    return (2.0 * jnp.eye(NODES, dtype=jnp.float32)[None] + offdiag).astype(jnp.bfloat16)


def plant(result, own_key, low, top_value):
    index_at = [jax.random.randint(jax.random.fold_in(own_key, axis), (), 0, length) for axis, length in enumerate(result.shape)]
    longest = result.shape.index(max(result.shape))
    neighbour = index_at[:longest] + [(index_at[longest] + 1) % result.shape[longest]] + index_at[longest + 1:]
    return result.at[tuple(index_at)].set(low).at[tuple(neighbour)].set(top_value)


def block_scale(key, dims, cuts, least, top_value):
    level = 1.0
    for dim, blocks in cuts:
        heights = jax.random.uniform(jax.random.fold_in(jax.random.fold_in(key, 6), dim), (blocks,), jnp.float32, least / len(cuts), top_value / len(cuts))
        level = level * jnp.repeat(jnp.exp(heights), dims[dim] // blocks).reshape((-1,) + (1,) * (len(dims) - 1 - dim))
    return level


def routed_block(stream_key, own, number, rows, amount, top, bound, lean):
    ranking = jax.random.permutation(stream_key, amount)
    packed, ordinary = shares(amount, rows * top, bound, lean, True), shares(amount, rows * top, bound, lean, False)
    places = jnp.arange(amount)

    def named(sizes, offset_by):
        used = int((sizes > 0).sum())
        fixed = max(1, used // 4)
        passed = fixed + (places - fixed + offset_by * (used - fixed)) % max(1, amount - fixed)
        return jnp.zeros((amount,), jnp.int32).at[ranking[jnp.where(places < fixed, places, passed)]].set(jnp.asarray(sizes, jnp.int32))

    sizes = jnp.where(number % 4 == 0, named(packed, number // 4), named(ordinary, number - number // 4 - 1))
    mixed = jax.random.permutation(jax.random.fold_in(own, 3), amount)
    donor, sink = mixed[0:amount // 2 * 2:2], mixed[1:amount // 2 * 2:2]
    room = jnp.minimum(sizes[donor] - 1, bound - sizes[sink]) // 2
    room = jnp.where((donor == ranking[0]) | (sink == ranking[0]) | (sizes[sink] == 0), 0, jnp.maximum(room, 0))
    passed = jax.random.randint(jax.random.fold_in(own, 4), (amount // 2,), 0, 1 << 20) % (room + 1)
    sizes = sizes.at[donor].add(-passed).at[sink].add(passed)
    labels = jnp.searchsorted(jnp.cumsum(sizes), jnp.arange(rows * top), side="right").astype(jnp.int32)
    grid = labels.reshape(top, rows).T
    grid = grid[jax.random.permutation(jax.random.fold_in(own, 1), rows)]
    offset_by = jax.random.randint(jax.random.fold_in(own, 2), (rows, 1), 0, top)
    return jnp.take_along_axis(grid, (jnp.arange(top)[None, :] + offset_by) % top, axis=1)


def shares(count, total, most, skew, full):
    loads = [(1 << 20) // math.isqrt(rank ** skew) + 1 for rank in range(1, count + 1)]
    largest = most if full else min(most, max(-(-total // count), total * loads[0] // sum(loads)))
    least = 1 if total - largest >= count - 1 else 0
    counts, spare = [largest] + [least] * (count - 1), total - largest - least * (count - 1)
    while spare > 0:
        movable = [i for i in range(1, count) if counts[i] < largest] or [i for i in range(1, count) if counts[i] < most]
        whole, left = sum([loads[i] for i in movable]), spare
        for i in movable:
            addition = min(most - counts[i], max(1, left * loads[i] // whole), spare)
            counts[i] = counts[i] + addition
            spare = spare - addition
    return np.array(counts)


def gaussian(key, shape, width, most, pieces=(), kind=jnp.bfloat16):
    entries = width * jax.random.normal(key, shape, jnp.float32)
    if pieces:
        entries = entries * block_scale(key, shape, pieces, -0.22, 0.18)
    return jnp.clip(entries, -most, most).astype(kind)


def setup_inputs(seed: int = 0) -> dict:
    key_list = jax.random.split(jax.random.key(seed), 15)
    density = jnp.clip(jnp.exp(math.log(2.0) - 1.3862944 * jax.random.uniform(key_list[0], (NX, CY, CZ), jnp.float32) ** block_scale(key_list[0], (NX, CY, CZ), ((0, 128),), -0.2, 0.2)), 0.5, 2.0)
    velocity = gaussian(key_list[1], (3, NX, CY, CZ), 0.3, 0.75, ((1, 128),), jnp.float32)
    pressure = jnp.clip(jnp.exp(math.log(2.0) - 1.3862944 * jax.random.uniform(key_list[2], (NX, CY, CZ), jnp.float32) ** block_scale(key_list[2], (NX, CY, CZ), ((0, 128),), -0.2, 0.2)), 0.5, 2.0)
    rbf_blocks = gaussian(key_list[3], (NBT, NODES, NODES), NODES ** -0.5, 0.5, ((0, 128),))
    correlation = plant(jax.random.randint(key_list[4], (NBT, NODES), 0, CX * CY), jax.random.fold_in(key_list[4], 1), 0, (CX * CY) - 1).astype(jnp.int32)
    normals = gaussian(key_list[5], (NBT, 3, NODES), 1.0, 6.0, ((0, 128),), jnp.float32)
    routes_keys = jax.random.split(jax.random.fold_in(key_list[6], 1), NBT // NB)
    routes_turns = jax.random.permutation(jax.random.fold_in(key_list[6], 3), NBT // NB)
    routes = jax.vmap(lambda own, number: routed_block(jax.random.fold_in(key_list[6], 2), own, number, NB, DEVICES, 1, CAP, 2))(routes_keys, routes_turns).reshape((NBT, 1))
    targets = plant(jax.random.randint(key_list[7], (NBT,), 0, NS), jax.random.fold_in(key_list[7], 1), 0, NS - 1).astype(jnp.int32)
    stiffness = draw_stiffness(jax.random.fold_in(key_list[14], 71), 0)
    coupling = gaussian(key_list[9], (NST, NODES, NODES), NODES ** -0.5, 0.5, ((0, 128),))
    inverse_diag = jnp.clip(1.0 + 0.1 * jax.random.normal(key_list[10], (NST, 3, NODES), jnp.float32), 0.5, 1.5)
    displacement = draw_displacement(jax.random.fold_in(key_list[14], 71), 0)
    diff_res = draw_diff_res(jax.random.fold_in(key_list[14], 71), 0)
    diff_disp = gaussian(key_list[13], (M, NST, 3, NODES), 0.4, 2.4, ((1, 128),), jnp.float32)
    return {"density": density, "velocity": velocity, "pressure": pressure, "rbf_blocks": rbf_blocks, "correlation": correlation, "normals": normals, "routes": routes, "targets": targets, "stiffness": stiffness, "coupling": coupling, "inverse_diag": inverse_diag, "displacement": displacement, "diff_res": diff_res, "diff_disp": diff_disp}


ratio_heat = 1.4
step_ratio = 0.03

def euler_flux(state, normal_axis):
    dens = state[0]
    vel = state[1:4] / dens
    press = (ratio_heat - 1.0) * (state[4] - 0.5 * dens * lax.optimization_barrier(jnp.sum(vel * vel, axis=0)))
    normal_speed = vel[normal_axis]
    rows = [dens * normal_speed]
    for comp in range(3):
        moment = state[1 + comp] * normal_speed
        if comp == normal_axis:
            moment = moment + press
        rows.append(moment)
    rows.append((state[4] + press) * normal_speed)
    wave_speed = jnp.abs(normal_speed) + jnp.sqrt(ratio_heat * press / dens)
    return (jnp.stack(rows, axis=0), wave_speed)

def rusanov(left_state, right_state, normal_axis):
    flux_left, speed_left = euler_flux(left_state, normal_axis)
    flux_right, speed_right = euler_flux(right_state, normal_axis)
    return 0.5 * (flux_left + flux_right) - 0.5 * jnp.maximum(speed_left, speed_right) * (right_state - left_state)

def conserve(density, velocity, pressure):
    energy = pressure / (ratio_heat - 1.0) + 0.5 * density * lax.optimization_barrier(jnp.sum(velocity * velocity, axis=0))
    return jnp.concatenate([density[None], density[None] * velocity, energy[None]], axis=0)

def advance(padded, conserved):
    face_x = rusanov(padded[:, :-1], padded[:, 1:], 0)
    divergence = face_x[:, 1:] - face_x[:, :-1]
    face_y = rusanov(conserved, jnp.roll(conserved, -1, axis=2), 1)
    divergence = divergence + face_y - jnp.roll(face_y, 1, axis=2)
    mirror_sign = jnp.array([1.0, 1.0, 1.0, -1.0, 1.0], dtype=conserved.dtype)[:, None, None, None]
    padded_z = jnp.concatenate([conserved[..., :1] * mirror_sign, conserved, conserved[..., -1:]], axis=3)
    face_z = rusanov(padded_z[..., :-1], padded_z[..., 1:], 2)
    divergence = divergence + face_z[..., 1:] - face_z[..., :-1]
    return conserved - step_ratio * divergence

def wall_pressure(state):
    bottom = state[..., 0]
    return (ratio_heat - 1.0) * (bottom[4] - 0.5 * lax.optimization_barrier(jnp.sum(bottom[1:4] * bottom[1:4], axis=0)) / bottom[0])

def cho_apply(gram, projected):
    factor = jnp.linalg.cholesky(gram)
    middle = lax.linalg.triangular_solve(factor, projected[:, None], left_side=True, lower=True)
    return lax.linalg.triangular_solve(factor, middle, left_side=True, lower=True, transpose_a=True)[:, 0]

def reference(density, velocity, pressure, rbf_blocks, correlation, normals, routes, targets, stiffness, coupling, inverse_diag, displacement, diff_res, diff_disp):
    row_offsets = jnp.arange(CX + 2, dtype=jnp.int32)

    def slab_step(index, carry):
        fluid_all, wall_all = carry
        slab_index = jnp.asarray(index).astype(jnp.int32)
        start = (slab_index * CX).astype(jnp.int32)
        row_ids = ((start - 1 + row_offsets) % NX).astype(jnp.int32)
        piece = conserve(jnp.take(density, row_ids, axis=0), jnp.take(velocity, row_ids, axis=1), jnp.take(pressure, row_ids, axis=0))
        slab = advance(piece, piece[:, 1:-1])
        fluid_all = lax.dynamic_update_slice_in_dim(fluid_all, slab, start, 1)
        wall_all = lax.dynamic_update_slice_in_dim(wall_all, wall_pressure(slab).reshape(1, CX * CY), slab_index, 0)
        return (fluid_all, wall_all)
    fluid_start = jnp.zeros((5, NX, CY, CZ), jnp.float32)
    wall_start = jnp.zeros((DEVICES, CX * CY), jnp.float32)
    fluid_next, wall_rows = lax.fori_loop(0, DEVICES, slab_step, (fluid_start, wall_start))

    def map_loads(element):
        wall_row, indices, normal_rows, kernels = element
        weighted = (wall_row[indices][:, None, :] * normal_rows).astype(jnp.bfloat16)
        return jnp.einsum('bci,bij->bcj', weighted.astype(jnp.float32), kernels.astype(jnp.float32))
    block_load = lax.map(map_loads, (wall_rows, correlation.reshape(DEVICES, NB, NODES), normals.reshape(DEVICES, NB, 3, NODES), rbf_blocks.reshape(DEVICES, NB, NODES, NODES)))
    block_load = block_load.reshape(NBT, 3, NODES)
    solid_ids = (routes[:, 0] * NS + targets).astype(jnp.int32)
    solid_load = jax.ops.segment_sum(block_load, solid_ids, num_segments=NST)
    disp_half = displacement.astype(jnp.bfloat16)
    earlier = jnp.concatenate([jnp.zeros((1, 3, NODES), jnp.bfloat16), disp_half[:-1]], axis=0)
    solid_res = jnp.einsum('bcj,bij->bci', disp_half.astype(jnp.float32), stiffness.astype(jnp.float32))
    solid_res = solid_res + jnp.einsum('bcj,bij->bci', earlier.astype(jnp.float32), coupling.astype(jnp.float32)) - solid_load
    coupling_res = -inverse_diag * solid_res
    gram = jnp.einsum('mbcj,nbcj->mn', diff_res, diff_res, precision=lax.Precision.HIGHEST)
    projected = jnp.einsum('mbcj,bcj->m', diff_res, coupling_res, precision=lax.Precision.HIGHEST)
    mixing = -cho_apply(gram, projected)
    disp_next = displacement + coupling_res + jnp.einsum('mbcj,m->bcj', diff_disp, mixing, precision=lax.Precision.HIGHEST)
    reply = disp_next.astype(jnp.bfloat16)[solid_ids]

    def map_motion(element):
        kernels, rows = element
        return jnp.einsum('bij,bcj->bci', kernels.astype(jnp.float32), rows.astype(jnp.float32))
    wall_motion = lax.map(map_motion, (rbf_blocks.reshape(DEVICES, NB, NODES, NODES), reply.reshape(DEVICES, NB, 3, NODES)))
    return (fluid_next, disp_next, wall_motion.reshape(NBT, 3, NODES))
```

```python
import functools

import jax
import jax.numpy as jnp
from jax import lax
from jax.experimental import pallas as pl
from jax.experimental.pallas import tpu as pltpu
from jax.sharding import PartitionSpec as P

AXES = ("group", "dev")
ratio_heat = 1.4
step_ratio = 0.03
f32 = jnp.float32
bf16 = jnp.bfloat16


def iota(shape, dim):
    return lax.broadcasted_iota(jnp.int32, shape, dim)


def call(kernel, out, *args, scratch=(), limit=48):
    return pl.pallas_call(
        kernel,
        out_shape=out,
        scratch_shapes=list(scratch),
        compiler_params=pltpu.CompilerParams(vmem_limit_bytes=limit * 2**20),
        name=kernel.__name__,
    )(*args)


def shape(dims, dtype=f32):
    return jax.ShapeDtypeStruct(dims, dtype)


def conserve(cell):
    dens, v0, v1, v2, press = cell
    kinetic = v0 * v0 + v1 * v1 + v2 * v2
    energy = press * (1.0 / (ratio_heat - 1.0)) + 0.5 * dens * kinetic
    return (dens, dens * v0, dens * v1, dens * v2, energy)


def sound(cell):
    return jnp.sqrt(ratio_heat * cell[4] / cell[0])


def with_speed(cell):
    return (cell, conserve(cell), sound(cell))


def euler_flux(state, axis):
    cell, cons, speed = state
    normal = cell[1 + axis]
    rows = [cons[1 + axis]]
    for comp in range(3):
        moment = cons[1 + comp] * normal
        rows.append(moment + cell[4] if comp == axis else moment)
    rows.append((cons[4] + cell[4]) * normal)
    return rows, jnp.abs(normal) + speed


def rusanov(left, right, axis):
    flux_left, speed_left = euler_flux(left, axis)
    flux_right, speed_right = euler_flux(right, axis)
    top = jnp.maximum(speed_left, speed_right)
    return [
        0.5 * (a + b - top * (r - l))
        for a, b, l, r in zip(flux_left, flux_right, left[1], right[1])
    ]


def wall_flux(state):
    cell, cons, speed = state
    return cons[3] * cell[3] + cell[4] - (jnp.abs(cell[3]) + speed) * cons[3]


def edges(dens_ref, vel_ref, press_ref, disp_ref, send_ref, second_ref, bulk_ref):
    depth, lanes = dens_ref.shape[1:]
    wide = send_ref.shape[1]
    lane = iota((depth, lanes), 1)
    packed = jnp.ones((depth, lanes), f32)
    rows = [dens_ref[0], vel_ref[0, 0], vel_ref[1, 0], vel_ref[2, 0], press_ref[0]]
    for i, row in enumerate(rows):
        bulk_ref[i] = row.astype(bf16)
        moved = row if i == 0 else pltpu.roll(row, 2 * i, 1)
        packed = jnp.where((lane >> 1) == i, moved, packed)
    packed = jnp.concatenate([packed, jnp.ones((wide - depth, lanes), f32)], axis=0)
    turned = packed.T
    last = disp_ref.shape[1] - 1
    for i in range(5):
        send_ref[i : i + 1, :] = turned[2 * i : 2 * i + 1, :]
        second_ref[i : i + 1, :] = turned[2 * i + 1 : 2 * i + 2, :]
    nodes = disp_ref.shape[2]
    for c in range(3):
        send_ref[5:6, c * nodes : (c + 1) * nodes] = disp_ref[c, last : last + 1, :]
    send_ref[6:8, :] = jnp.zeros((2, wide), f32)
    second_ref[5:8, :] = jnp.zeros((3, wide), f32)


def fluid(dens_ref, vel_ref, press_ref, below_ref, above_ref, next_ref):
    depth, lanes = dens_ref.shape[1:]
    rows = 16
    sub = iota((rows, lanes), 0)
    lane = iota((rows, lanes), 1)

    def load(at):
        return (
            dens_ref[0, at, :],
            vel_ref[0, 0, at, :],
            vel_ref[1, 0, at, :],
            vel_ref[2, 0, at, :],
            press_ref[0, at, :],
        )

    def step(i, carried):
        start = pl.multiple_of(i * rows, rows)
        after = pl.multiple_of(jnp.where(start + rows == depth, 0, start + rows), 8)
        at = pl.ds(start, rows)
        cell = load(at)
        ahead = load(pl.ds(after, 8))
        me = with_speed(cell)
        below = with_speed([below_ref[q, at, :].astype(f32) for q in range(5)])
        above = with_speed([above_ref[q, at, :].astype(f32) for q in range(5)])
        total = [
            b - a for a, b in zip(rusanov(below, me, 0), rusanov(me, above, 0))
        ]
        beside = with_speed(
            [
                jnp.where(sub == rows - 1, n[0:1, :], pltpu.roll(x, rows - 1, 0))
                for x, n in zip(cell, ahead)
            ]
        )
        face = rusanov(me, beside, 1)
        total = [
            t + f - jnp.where(sub == 0, c, pltpu.roll(f, 1, 0))
            for t, f, c in zip(total, face, carried)
        ]
        carried = tuple(f[rows - 1 : rows, :] for f in face)
        over = with_speed(
            [jnp.where(lane == lanes - 1, x, pltpu.roll(x, lanes - 1, 1)) for x in cell]
        )
        face = rusanov(me, over, 2)
        wall = wall_flux(me)
        for q in range(5):
            lower = jnp.where(
                lane == 0, wall if q == 3 else 0.0, pltpu.roll(face[q], 1, 1)
            )
            next_ref[q, 0, at, :] = me[1][q] - step_ratio * (total[q] + face[q] - lower)
        return carried

    first = with_speed([x[0:1, :] for x in load(pl.ds(0, 8))])
    last = with_speed([x[7:8, :] for x in load(pl.ds(depth - 8, 8))])
    lax.fori_loop(0, depth // rows, step, tuple(rusanov(last, first, 1)))


def wall_pressure(depth, own, second, below, above):
    wide = own[0].shape[1]
    lane = iota((1, wide), 1)
    me = with_speed(own)
    total = [
        b - a
        for a, b in zip(
            rusanov(with_speed(below), me, 0), rusanov(me, with_speed(above), 0)
        )
    ]

    def up(x):
        return jnp.where(lane == depth - 1, x[:, 0:1], pltpu.roll(x, wide - 1, 1))

    def down(x):
        return jnp.where(lane == 0, x[:, depth - 1 : depth], pltpu.roll(x, 1, 1))

    face = rusanov(me, with_speed([up(x) for x in own]), 1)
    total = [t + f - down(f) for t, f in zip(total, face)]
    face = rusanov(me, with_speed(second), 2)
    total = [t + f for t, f in zip(total, face)]
    total[3] = total[3] - wall_flux(me)
    q = [c - step_ratio * t for c, t in zip(me[1], total)]
    return (ratio_heat - 1.0) * (
        q[4] - 0.5 * (q[1] * q[1] + q[2] * q[2] + q[3] * q[3]) / q[0]
    )


def routing(routes_ref, targets_ref, diff_ref, scatter_ref, pick_ref, tag_ref, gram_ref):
    count = routes_ref.shape[1]
    spread, taken = scatter_ref.shape
    peers = tag_ref.shape[0]
    ii, jj = iota((count, count), 0), iota((count, count), 1)
    route_row = jnp.broadcast_to(routes_ref[...], (count, count)).astype(f32)
    target_row = jnp.broadcast_to(targets_ref[...], (count, count)).astype(f32)
    route_col = jnp.sum(jnp.where(ii == jj, route_row, 0.0), axis=1, keepdims=True)
    target_col = jnp.sum(jnp.where(ii == jj, target_row, 0.0), axis=1, keepdims=True)
    same = jnp.where(route_col == route_row, 1.0, 0.0)
    place_col = jnp.sum(jnp.where(jj < ii, same, 0.0), axis=1, keepdims=True)
    place_row = jnp.sum(jnp.where(ii < jj, same, 0.0), axis=0, keepdims=True)
    slot_col = route_col * 8.0 + place_col * 3.0
    slot_row = route_row[0:1, :] * 8.0 + place_row * 3.0
    own = (iota((count, taken), 1) >> 2) == iota((count, taken), 0)
    comp = iota((1, taken), 1) & 3
    at_row = jnp.sum(jnp.where(own, slot_col, 0.0), axis=0, keepdims=True)
    at_row = jnp.where(comp < 3, at_row + comp.astype(f32), -1.0)
    scatter_ref[...] = jnp.where(
        iota((spread, taken), 0).astype(f32) == at_row, 1.0, 0.0
    ).astype(bf16)
    own = (iota((taken, count), 0) >> 2) == iota((taken, count), 1)
    comp = iota((taken, 1), 0) & 3
    at_col = jnp.sum(jnp.where(own, slot_row, 0.0), axis=1, keepdims=True)
    at_col = jnp.where(comp < 3, at_col + comp.astype(f32), -1.0)
    pick_ref[...] = jnp.where(
        iota((taken, spread), 1).astype(f32) == at_col, 1.0, 0.0
    ).astype(bf16)
    to_peer = jnp.where(
        iota((peers, count), 0).astype(f32) == route_row[0:1, :], 1.0, 0.0
    )
    named = jnp.where(
        iota((count, tag_ref.shape[1]), 1).astype(f32) == place_col, target_col + 1.0, 0.0
    )
    tag_ref[...] = (
        jnp.dot(to_peer.astype(bf16), named.astype(bf16), preferred_element_type=f32) - 1.0
    )
    columns = diff_ref.shape[0]
    lanes = diff_ref.shape[3]
    sums = {}
    for m in range(columns):
        for n in range(m, columns):
            part = jnp.sum(diff_ref[m] * diff_ref[n], axis=0)
            sums[m, n] = jnp.sum(part, axis=0, keepdims=True)
    stacked = jnp.concatenate(
        [sums[min(m, n), max(m, n)] for m in range(columns) for n in range(columns)], axis=0
    )
    col = jnp.sum(stacked, axis=1, keepdims=True)
    diag = iota((columns * columns, lanes), 0) == iota((columns * columns, lanes), 1)
    gram_ref[...] = jnp.sum(jnp.where(diag, col, 0.0), axis=0, keepdims=True)


def thirds(value):
    high = value.astype(bf16)
    rest = value - high.astype(f32)
    middle = rest.astype(bf16)
    return high, middle, (rest - middle.astype(f32)).astype(bf16)


def exact_dot(onehot, value):
    return sum(jnp.dot(onehot, part, preferred_element_type=f32) for part in thirds(value))


def pick_half(both):
    lanes = both.shape[1] // 2
    return jnp.where(iota((8, lanes), 0) < 4, both[:, :lanes], both[:, lanes:])


def nt_dot(a, b):
    return lax.dot_general(a, b, (((1,), (1,)), ((), ())), preferred_element_type=f32)


def loads(
    depth, own_ref, second_ref, below_ref, above_ref, corr_ref, normals_ref, rbf_ref,
    scatter_ref, tag_ref, gram_ref, send_ref, weighted, mapped,
):
    def cell(ref):
        return [ref[i : i + 1, :] for i in range(5)]

    wall = wall_pressure(depth, cell(own_ref), cell(second_ref), cell(below_ref), cell(above_ref))
    count, nodes = corr_ref.shape
    at = corr_ref[...]
    within, part = at & (nodes - 1), at >> (nodes.bit_length() - 1)
    found = jnp.zeros((count, nodes), f32)
    for k in range(wall.shape[1] // nodes):
        table = jnp.broadcast_to(wall[:, k * nodes : (k + 1) * nodes], (count, nodes))
        got = jnp.take_along_axis(table, within, axis=1, mode="promise_in_bounds")
        found = jnp.where(part == k, got, found)
    for c in range(3):
        weighted[pl.ds(c, count, stride=4), :] = found * normals_ref[c]
    weighted[pl.ds(3, count, stride=4), :] = jnp.zeros((count, nodes), f32)
    for k in range(count // 2):
        both = jnp.concatenate([rbf_ref[2 * k], rbf_ref[2 * k + 1]], axis=1)
        left = weighted[8 * k : 8 * k + 8, :].astype(bf16)
        mapped[8 * k : 8 * k + 8, :] = pick_half(
            jnp.dot(left, both, preferred_element_type=f32)
        )
    send_ref[...] = exact_dot(scatter_ref[...], mapped[...])
    peers = tag_ref.shape[0]
    send_ref[pl.ds(6, peers, stride=8), :] = tag_ref[...]
    send_ref[pl.ds(7, peers, stride=8), :] = jnp.broadcast_to(gram_ref[...], tag_ref.shape)


def solid(keep_ref, disp_ref, below_ref, stiff_ref, coup_ref, out_ref, here, prior, made):
    count, nodes = disp_ref.shape[1:]
    for c in range(3):
        here[pl.ds(c, count, stride=4), :] = disp_ref[c]
        prior[pl.ds(4 + c, count, stride=4), :] = disp_ref[c]
        first = below_ref[5:6, c * nodes : (c + 1) * nodes]
        prior[c : c + 1, :] = jnp.where(keep_ref[0] > 0, first, 0.0)
    here[pl.ds(3, count, stride=4), :] = jnp.zeros((count, nodes), f32)
    prior[pl.ds(3, count + 1, stride=4), :] = jnp.zeros((count + 1, nodes), f32)
    for k in range(count // 2):
        rows = slice(8 * k, 8 * k + 8)
        left = jnp.concatenate([here[rows, :], prior[rows, :]], axis=1).astype(bf16)
        right = jnp.concatenate(
            [
                jnp.concatenate([stiff_ref[2 * k], stiff_ref[2 * k + 1]], axis=0),
                jnp.concatenate([coup_ref[2 * k], coup_ref[2 * k + 1]], axis=0),
            ],
            axis=1,
        )
        made[rows, :] = pick_half(nt_dot(left, right))
    for c in range(3):
        out_ref[c] = made[pl.ds(c, count, stride=4), :]


def residual(got_ref, kd_ref, inv_ref, disp_ref, diff_ref, base_ref, share_ref):
    count, nodes = disp_ref.shape[1:]
    peers = share_ref.shape[0]
    turned = got_ref[pl.ds(6, peers, stride=8), :].T
    block = iota((count, peers), 0).astype(f32)
    chosen = jnp.concatenate(
        [jnp.where(block == turned[i : i + 1, :], 1.0, 0.0) for i in range(2)], axis=1
    ).astype(bf16)
    res = []
    for c in range(3):
        rows = jnp.concatenate(
            [got_ref[pl.ds(c + 3 * i, peers, stride=8), :] for i in range(2)], axis=0
        )
        part = -inv_ref[c] * (kd_ref[c] - exact_dot(chosen, rows))
        base_ref[c] = disp_ref[c] + part
        res.append(part)
    columns = diff_ref.shape[0]
    sums = []
    for m in range(columns):
        part = sum(diff_ref[m, c] * res[c] for c in range(3))
        sums.append(jnp.sum(part, axis=0, keepdims=True))
    col = jnp.sum(jnp.concatenate(sums, axis=0), axis=1, keepdims=True)
    diag = iota((columns, nodes), 0) == iota((columns, nodes), 1)
    row = jnp.sum(jnp.where(diag, col, 0.0), axis=0, keepdims=True)
    share_ref[...] = jnp.broadcast_to(row, share_ref.shape)


def factor(blocks, got_ref, inverse_ref, serve_ref):
    spread, lanes = serve_ref.shape
    peers = spread // 8
    row = iota((8, lanes), 0)
    lane = iota((8, lanes), 1)
    second = row >= 3
    kept = ((lane // blocks) == jnp.where(second, row - 3, row)) & (row < 6)
    wanted = jnp.where(kept, lane % blocks, -2).astype(f32)
    for d in range(peers):
        tags = got_ref[8 * d + 6 : 8 * d + 7, :]
        tag = jnp.where(second, tags[:, 1:2], tags[:, 0:1])
        serve_ref[8 * d : 8 * d + 8, :] = jnp.where(tag == wanted, 1.0, 0.0).astype(bf16)
    total = jnp.sum(got_ref[pl.ds(7, peers, stride=8), :], axis=0, keepdims=True)
    n = 8
    gram = jnp.concatenate(
        [total if m == 0 else pltpu.roll(total, lanes - n * m, 1) for m in range(n)], axis=0
    )
    work = jnp.where(lane < n, gram, jnp.where(lane == row + n, 1.0, 0.0))
    for k in range(n):
        pivot = work[k : k + 1, :] * lax.rsqrt(work[k : k + 1, k : k + 1])
        below = work[:, k : k + 1] * lax.rsqrt(work[k : k + 1, k : k + 1])
        work = jnp.where(row == k, pivot, jnp.where(row > k, work - below * pivot, work))
    inverse_ref[...] = jnp.where(lane < n, pltpu.roll(work, lanes - n, 1), 0.0)


def update(share_ref, inverse_ref, base_ref, dd_ref, serve_ref, next_ref, reply_ref):
    projected = jnp.sum(share_ref[...], axis=0, keepdims=True)
    inverse = inverse_ref[...]
    middle = jnp.sum(inverse * projected, axis=1, keepdims=True)
    mixing = -jnp.sum(inverse * middle, axis=0, keepdims=True)
    rows = []
    for c in range(3):
        value = base_ref[c]
        for m in range(dd_ref.shape[0]):
            value = value + mixing[:, m : m + 1] * dd_ref[m, c]
        next_ref[c] = value
        rows.append(value)
    blocks = jnp.concatenate(rows, axis=0).astype(bf16)
    spare = serve_ref.shape[1] - blocks.shape[0]
    blocks = jnp.concatenate([blocks, jnp.zeros((spare, blocks.shape[1]), bf16)], axis=0)
    reply_ref[...] = jnp.dot(
        serve_ref[...], blocks, preferred_element_type=f32
    ).astype(bf16)


def motion(back_ref, pick_ref, rbf_ref, out_ref, picked, made):
    count = rbf_ref.shape[0]
    picked[...] = jnp.dot(pick_ref[...], back_ref[...], preferred_element_type=f32)
    for k in range(count // 2):
        rows = slice(8 * k, 8 * k + 8)
        both = jnp.concatenate([rbf_ref[2 * k], rbf_ref[2 * k + 1]], axis=0)
        made[rows, :] = pick_half(nt_dot(picked[rows, :].astype(bf16), both))
    for c in range(3):
        out_ref[c] = made[pl.ds(c, count, stride=4), :]


def exchange(value):
    return lax.all_to_all(value, AXES, split_axis=0, concat_axis=0, tiled=True)


def on_device(
    density, velocity, pressure, rbf, correlation, normals, routes, targets,
    stiffness, coupling, inverse_diag, displacement, diff_res, diff_disp,
):
    peers = lax.axis_size(AXES)
    depth, lanes = density.shape[1:]
    wide = -(-depth // 128) * 128
    count, nodes = correlation.shape
    blocks = displacement.shape[0]
    columns = diff_res.shape[0]
    normals, inverse_diag, displacement = (
        jnp.transpose(x, (1, 0, 2)) for x in (normals, inverse_diag, displacement)
    )
    diff_res, diff_disp = (jnp.transpose(x, (0, 2, 1, 3)) for x in (diff_res, diff_disp))
    ring = [(i, (i + 1) % peers) for i in range(peers)]
    back = [(j, i) for i, j in ring]

    own, second, bulk = call(
        edges,
        [shape((8, wide)), shape((8, wide)), shape((5, depth, lanes), bf16)],
        density, velocity, pressure, displacement,
    )
    below = lax.ppermute(own, AXES, ring)
    above = lax.ppermute(own, AXES, back)
    bulk_below = lax.ppermute(bulk, AXES, ring)
    bulk_above = lax.ppermute(bulk, AXES, back)
    scatter, pick, tag, gram = call(
        routing,
        [
            shape((8 * peers, 4 * count), bf16),
            shape((4 * count, 8 * peers), bf16),
            shape((peers, nodes)),
            shape((1, nodes)),
        ],
        routes.reshape(1, count), targets.reshape(1, count), diff_res,
    )
    kernel = functools.partial(loads, depth)
    kernel.__name__ = "loads"
    sent = call(
        kernel,
        shape((8 * peers, nodes)),
        own, second, below, above, correlation, normals, rbf, scatter, tag, gram,
        scratch=[pltpu.VMEM((4 * count, nodes), f32)] * 2,
    )
    got = exchange(sent.reshape(peers, 8, nodes)).reshape(8 * peers, nodes)
    keep = (lax.axis_index(AXES) > 0).astype(jnp.int32).reshape(1)
    stiff_call = pl.pallas_call(
        solid,
        out_shape=shape((3, blocks, nodes)),
        in_specs=[pl.BlockSpec(memory_space=pltpu.SMEM)]
        + [pl.BlockSpec(memory_space=pltpu.VMEM)] * 4,
        scratch_shapes=[
            pltpu.VMEM((4 * blocks, nodes), f32),
            pltpu.VMEM((4 * blocks + 8, nodes), f32),
            pltpu.VMEM((4 * blocks, nodes), f32),
        ],
        compiler_params=pltpu.CompilerParams(vmem_limit_bytes=48 * 2**20),
        name="solid",
    )
    product = stiff_call(keep, displacement, below, stiffness, coupling)
    base, share = call(
        residual,
        [shape((3, blocks, nodes)), shape((peers, nodes))],
        got, product, inverse_diag, displacement, diff_res,
    )
    shares = exchange(share)
    kernel = functools.partial(factor, blocks)
    kernel.__name__ = "factor"
    inverse, serve = call(
        kernel, [shape((columns, nodes)), shape((8 * peers, nodes), bf16)], got
    )
    disp_next, reply = call(
        update,
        [shape((3, blocks, nodes)), shape((8 * peers, nodes), bf16)],
        shares, inverse, base, diff_disp, serve,
    )
    returned = exchange(reply.reshape(peers, 8, nodes)).reshape(8 * peers, nodes)
    fluid_next = call(
        fluid,
        shape((5, 1, depth, lanes)),
        density, velocity, pressure, bulk_below, bulk_above,
    )
    wall_motion = call(
        motion,
        shape((3, count, nodes)),
        returned, pick, rbf,
        scratch=[pltpu.VMEM((4 * count, nodes), f32)] * 2,
    )
    return (
        fluid_next,
        jnp.transpose(disp_next, (1, 0, 2)),
        jnp.transpose(wall_motion, (1, 0, 2)),
    )


def solution(mesh):
    rows = P(AXES, None, None)
    inner = P(None, AXES, None, None)
    return jax.shard_map(
        on_device,
        mesh=mesh,
        in_specs=(
            rows, inner, rows, rows, P(AXES, None), rows, P(AXES, None), P(AXES),
            rows, rows, rows, rows, inner, inner,
        ),
        out_specs=(inner, rows, rows),
        check_vma=False,
    )
```

```python
import functools

import jax
import jax.numpy as jnp
from jax import lax
from jax.experimental import pallas as pl
from jax.experimental.pallas import tpu as pltpu
from jax.sharding import PartitionSpec as P

AXES = ("group", "dev")
ratio_heat = 1.4
half_step = 0.5 * 0.03
f32 = jnp.float32
bf16 = jnp.bfloat16


def iota(shape, dim):
    return lax.broadcasted_iota(jnp.int32, shape, dim)


def call(kernel, out, *args, fetched=(), remote=(), scalars=(), scratch=(), limit=48):
    held = (*fetched, *remote)
    buffers = [pltpu.VMEM(args[i].shape, args[i].dtype) for i in fetched]
    if fetched:
        buffers.append(pltpu.SemaphoreType.DMA((len(fetched),)))
    args = [
        pltpu.with_memory_space_constraint(x, pltpu.HBM) if i in held else x
        for i, x in enumerate(args)
    ]
    return pl.pallas_call(
        kernel,
        out_shape=out,
        in_specs=[
            pl.BlockSpec(
                memory_space=pltpu.HBM
                if i in held
                else pltpu.SMEM
                if i in scalars
                else pltpu.VMEM
            )
            for i in range(len(args))
        ],
        scratch_shapes=buffers + list(scratch),
        compiler_params=pltpu.CompilerParams(vmem_limit_bytes=limit * 2**20),
        name=kernel.__name__,
    )(*args)


def fetch(sources, buffers, semaphores):
    copies = [
        pltpu.make_async_copy(source, buffer, semaphores.at[i])
        for i, (source, buffer) in enumerate(zip(sources, buffers))
    ]
    for copy in copies:
        copy.start()
    return copies


def shape(dims, dtype=f32):
    return jax.ShapeDtypeStruct(dims, dtype)


def conserve(cell):
    dens, v0, v1, v2, press = cell
    kinetic = v0 * v0 + v1 * v1 + v2 * v2
    energy = press * (1.0 / (ratio_heat - 1.0)) + 0.5 * dens * kinetic
    return (dens, dens * v0, dens * v1, dens * v2, energy)


def sound(cell):
    scaled = ratio_heat * cell[4]
    return scaled * lax.rsqrt(scaled * cell[0])


def with_speed(cell):
    return (cell, conserve(cell), sound(cell))


def euler_flux(state, axis):
    cell, cons, speed = state
    normal = cell[1 + axis]
    rows = [cons[1 + axis]]
    for comp in range(3):
        moment = cons[1 + comp] * normal
        rows.append(moment + cell[4] if comp == axis else moment)
    rows.append((cons[4] + cell[4]) * normal)
    return rows, jnp.abs(normal) + speed


def rusanov(left, right, axis):
    flux_left, speed_left = euler_flux(left, axis)
    flux_right, speed_right = euler_flux(right, axis)
    top = jnp.maximum(speed_left, speed_right)
    return [
        a + b - top * (r - l)
        for a, b, l, r in zip(flux_left, flux_right, left[1], right[1])
    ]


def divergence(left, me, right, axis):
    flux_left, speed_left = euler_flux(left, axis)
    flux_right, speed_right = euler_flux(right, axis)
    own = jnp.abs(me[0][1 + axis]) + me[2]
    low, high = jnp.maximum(speed_left, own), jnp.maximum(own, speed_right)
    return [
        b - a - high * (r - c) + low * (c - l)
        for a, b, l, c, r in zip(flux_left, flux_right, left[1], me[1], right[1])
    ]


def wall_flux(state):
    cell, cons, speed = state
    return 2.0 * (cons[3] * cell[3] + cell[4] - (jnp.abs(cell[3]) + speed) * cons[3])


def edges(
    dens_hbm, vel_hbm, press_hbm, disp_hbm, send_ref, second_ref,
    dens_ref, vel_ref, press_ref, disp_ref, semaphores,
):
    copies = fetch(
        (dens_hbm, vel_hbm, press_hbm, disp_hbm),
        (dens_ref, vel_ref, press_ref, disp_ref),
        semaphores,
    )
    depth, lanes = dens_ref.shape[1:]
    wide = send_ref.shape[1]
    lane = iota((depth, lanes), 1)
    packed = jnp.ones((depth, lanes), f32)
    rows = [
        (copies[0], dens_ref.at[0]),
        (copies[1], vel_ref.at[0, 0]),
        (None, vel_ref.at[1, 0]),
        (None, vel_ref.at[2, 0]),
        (copies[2], press_ref.at[0]),
    ]
    for i, (copy, ref) in enumerate(rows):
        if copy is not None:
            copy.wait()
        row = ref[...]
        moved = row if i == 0 else pltpu.roll(row, 2 * i, 1)
        packed = jnp.where((lane >> 1) == i, moved, packed)
    packed = jnp.concatenate([packed, jnp.ones((wide - depth, lanes), f32)], axis=0)
    turned = packed.T
    last = disp_ref.shape[1] - 1
    copies[3].wait()
    for i in range(5):
        send_ref[i : i + 1, :] = turned[2 * i : 2 * i + 1, :]
        second_ref[i : i + 1, :] = turned[2 * i + 1 : 2 * i + 2, :]
    nodes = disp_ref.shape[2]
    for c in range(3):
        send_ref[5:6, c * nodes : (c + 1) * nodes] = disp_ref[c, last : last + 1, :]
    send_ref[6:8, :] = jnp.zeros((2, wide), f32)
    second_ref[5:8, :] = jnp.zeros((3, wide), f32)


def fluid(
    dens_hbm, vel_hbm, press_hbm, below_hbm, above_hbm, next_ref,
    dens_ref, vel_ref, press_ref, below_ref, above_ref, semaphores,
):
    for copy in fetch(
        (dens_hbm, vel_hbm, press_hbm, below_hbm, above_hbm),
        (dens_ref, vel_ref, press_ref, below_ref, above_ref),
        semaphores,
    ):
        copy.wait()
    depth, lanes = dens_ref.shape[1:]
    rows = 16
    sub = iota((rows, lanes), 0)
    lane = iota((rows, lanes), 1)

    def load(at):
        return (
            dens_ref[0, at, :],
            vel_ref[0, 0, at, :],
            vel_ref[1, 0, at, :],
            vel_ref[2, 0, at, :],
            press_ref[0, at, :],
        )

    def step(i, carried):
        start = pl.multiple_of(i * rows, rows)
        after = pl.multiple_of(jnp.where(start + rows == depth, 0, start + rows), 8)
        at = pl.ds(start, rows)
        cell = load(at)
        ahead = load(pl.ds(after, 8))
        me = with_speed(cell)
        below = with_speed([below_ref[q, at, :].astype(f32) for q in range(5)])
        above = with_speed([above_ref[q, at, :].astype(f32) for q in range(5)])
        total = divergence(below, me, above, 0)
        beside = with_speed(
            [
                jnp.where(sub == rows - 1, n[0:1, :], pltpu.roll(x, rows - 1, 0))
                for x, n in zip(cell, ahead)
            ]
        )
        face = rusanov(me, beside, 1)
        total = [
            t + f - jnp.where(sub == 0, c, pltpu.roll(f, 1, 0))
            for t, f, c in zip(total, face, carried)
        ]
        carried = tuple(f[rows - 1 : rows, :] for f in face)
        over = with_speed(
            [jnp.where(lane == lanes - 1, x, pltpu.roll(x, lanes - 1, 1)) for x in cell]
        )
        face = rusanov(me, over, 2)
        wall = wall_flux(me)
        for q in range(5):
            lower = jnp.where(
                lane == 0, wall if q == 3 else 0.0, pltpu.roll(face[q], 1, 1)
            )
            next_ref[q, 0, at, :] = me[1][q] - half_step * (total[q] + face[q] - lower)
        return carried

    first = with_speed([x[0:1, :] for x in load(pl.ds(0, 8))])
    last = with_speed([x[7:8, :] for x in load(pl.ds(depth - 8, 8))])
    lax.fori_loop(0, depth // rows, step, tuple(rusanov(last, first, 1)))


def wall_pressure(depth, own, second, below, above):
    wide = own[0].shape[1]
    lane = iota((1, wide), 1)
    me = with_speed(own)
    total = divergence(with_speed(below), me, with_speed(above), 0)

    def up(x):
        return jnp.where(lane == depth - 1, x[:, 0:1], pltpu.roll(x, wide - 1, 1))

    def down(x):
        return jnp.where(lane == 0, x[:, depth - 1 : depth], pltpu.roll(x, 1, 1))

    face = rusanov(me, with_speed([up(x) for x in own]), 1)
    total = [t + f - down(f) for t, f in zip(total, face)]
    face = rusanov(me, with_speed(second), 2)
    total = [t + f for t, f in zip(total, face)]
    total[3] = total[3] - wall_flux(me)
    q = [c - half_step * t for c, t in zip(me[1], total)]
    return (ratio_heat - 1.0) * (
        q[4] - 0.5 * (q[1] * q[1] + q[2] * q[2] + q[3] * q[3]) / q[0]
    )


def routing(
    routes_hbm, targets_hbm, diff_hbm, dens_hbm, vel_hbm, press_hbm,
    corr_hbm, normals_hbm, rbf_hbm,
    scatter_ref, slot_ref, tag_ref, gram_ref, bulk_ref, corr_ref, normals_ref, rbf_ref,
    routes_ref, targets_ref, diff_ref, dens_ref, vel_ref, press_ref, semaphores, ahead,
):
    copies = fetch(
        (routes_hbm, targets_hbm, diff_hbm, dens_hbm, vel_hbm, press_hbm),
        (routes_ref, targets_ref, diff_ref, dens_ref, vel_ref, press_ref),
        semaphores,
    )
    later = fetch((corr_hbm, normals_hbm, rbf_hbm), (corr_ref, normals_ref, rbf_ref), ahead)
    copies[0].wait()
    copies[1].wait()
    count = routes_ref.shape[1]
    spread, taken = scatter_ref.shape
    peers = tag_ref.shape[0]
    ii, jj = iota((count, count), 0), iota((count, count), 1)
    route_row = jnp.broadcast_to(routes_ref[...], (count, count)).astype(f32)
    target_row = jnp.broadcast_to(targets_ref[...], (count, count)).astype(f32)
    route_col = jnp.sum(jnp.where(ii == jj, route_row, 0.0), axis=1, keepdims=True)
    target_col = jnp.sum(jnp.where(ii == jj, target_row, 0.0), axis=1, keepdims=True)
    same = jnp.where(route_col == route_row, 1.0, 0.0)
    place_col = jnp.sum(jnp.where(jj < ii, same, 0.0), axis=1, keepdims=True)
    place_row = jnp.sum(jnp.where(ii < jj, same, 0.0), axis=0, keepdims=True)
    slot_col = route_col * 8.0 + place_col * 3.0
    slot_row = route_row[0:1, :] * 8.0 + place_row * 3.0
    own = (iota((count, taken), 1) >> 2) == iota((count, taken), 0)
    comp = iota((1, taken), 1) & 3
    at_row = jnp.sum(jnp.where(own, slot_col, 0.0), axis=0, keepdims=True)
    at_row = jnp.where(comp < 3, at_row + comp.astype(f32), -1.0)
    scatter_ref[...] = jnp.where(
        iota((spread, taken), 0).astype(f32) == at_row, 1.0, 0.0
    ).astype(bf16)
    own = (iota((taken, count), 0) >> 2) == iota((taken, count), 1)
    comp = iota((taken, 1), 0) & 3
    at_col = jnp.sum(jnp.where(own, slot_row, 0.0), axis=1, keepdims=True)
    at_col = jnp.where(comp < 3, at_col + comp.astype(f32), -1.0)
    slot_ref[...] = at_col
    to_peer = jnp.where(
        iota((peers, count), 0).astype(f32) == route_row[0:1, :], 1.0, 0.0
    )
    named = jnp.where(
        iota((count, tag_ref.shape[1]), 1).astype(f32) == place_col, target_col + 1.0, 0.0
    )
    tag_ref[...] = (
        jnp.dot(to_peer.astype(bf16), named.astype(bf16), preferred_element_type=f32) - 1.0
    )
    copies[2].wait()
    columns = diff_ref.shape[0]
    lanes = diff_ref.shape[3]
    sums = {}
    for m in range(columns):
        for n in range(m, columns):
            part = jnp.sum(diff_ref[m] * diff_ref[n], axis=0)
            sums[m, n] = jnp.sum(part, axis=0, keepdims=True)
    stacked = jnp.concatenate(
        [sums[min(m, n), max(m, n)] for m in range(columns) for n in range(columns)], axis=0
    )
    col = jnp.sum(stacked, axis=1, keepdims=True)
    diag = iota((columns * columns, lanes), 0) == iota((columns * columns, lanes), 1)
    gram_ref[...] = jnp.sum(jnp.where(diag, col, 0.0), axis=0, keepdims=True)
    for copy in copies[3:] + later:
        copy.wait()
    bulk_ref[0] = dens_ref[0].astype(bf16)
    for c in range(3):
        bulk_ref[1 + c] = vel_ref[c, 0].astype(bf16)
    bulk_ref[4] = press_ref[0].astype(bf16)


def thirds(value):
    high = value.astype(bf16)
    rest = value - high.astype(f32)
    middle = rest.astype(bf16)
    return high, middle, (rest - middle.astype(f32)).astype(bf16)


def exact_dot(onehot, value):
    parts = jnp.concatenate(thirds(value), axis=1)
    made = jnp.dot(onehot, parts, preferred_element_type=f32)
    lanes = value.shape[1]
    return made[:, :lanes] + made[:, lanes : 2 * lanes] + made[:, 2 * lanes :]


def pick_half(both):
    lanes = both.shape[1] // 2
    return jnp.where(iota((8, lanes), 0) < 4, both[:, :lanes], both[:, lanes:])


def nt_dot(a, b):
    return lax.dot_general(a, b, (((1,), (1,)), ((), ())), preferred_element_type=f32)


def loads(
    depth, own_ref, second_ref, below_ref, above_ref, corr_ref, normals_ref, rbf_ref,
    scatter_ref, tag_ref, gram_ref, send_ref, weighted, mapped,
):
    def cell(ref):
        return [ref[i : i + 1, :] for i in range(5)]

    wall = wall_pressure(depth, cell(own_ref), cell(second_ref), cell(below_ref), cell(above_ref))
    count, nodes = corr_ref.shape
    at = corr_ref[...]
    within, part = at & (nodes - 1), at >> (nodes.bit_length() - 1)
    found = jnp.zeros((count, nodes), f32)
    for k in range(wall.shape[1] // nodes):
        table = jnp.broadcast_to(wall[:, k * nodes : (k + 1) * nodes], (count, nodes))
        got = jnp.take_along_axis(table, within, axis=1, mode="promise_in_bounds")
        found = jnp.where(part == k, got, found)
    for c in range(3):
        weighted[pl.ds(c, count, stride=4), :] = found * normals_ref[c]
    weighted[pl.ds(3, count, stride=4), :] = jnp.zeros((count, nodes), f32)
    for k in range(count // 2):
        both = jnp.concatenate([rbf_ref[2 * k], rbf_ref[2 * k + 1]], axis=1)
        left = weighted[8 * k : 8 * k + 8, :].astype(bf16)
        mapped[8 * k : 8 * k + 8, :] = pick_half(
            jnp.dot(left, both, preferred_element_type=f32)
        )
    send_ref[...] = exact_dot(scatter_ref[...], mapped[...])
    peers = tag_ref.shape[0]
    send_ref[pl.ds(6, peers, stride=8), :] = tag_ref[...]
    send_ref[pl.ds(7, peers, stride=8), :] = jnp.broadcast_to(gram_ref[...], tag_ref.shape)


def solid(
    keep_ref, disp_ref, below_ref, stiff_hbm, coup_hbm, out_ref,
    stiff_ref, coup_ref, semaphores, here, prior, made,
):
    copies = fetch((stiff_hbm, coup_hbm), (stiff_ref, coup_ref), semaphores)
    count, nodes = disp_ref.shape[1:]
    for c in range(3):
        here[pl.ds(c, count, stride=4), :] = disp_ref[c]
        prior[pl.ds(4 + c, count, stride=4), :] = disp_ref[c]
        first = below_ref[5:6, c * nodes : (c + 1) * nodes]
        prior[c : c + 1, :] = jnp.where(keep_ref[0] > 0, first, 0.0)
    here[pl.ds(3, count, stride=4), :] = jnp.zeros((count, nodes), f32)
    prior[pl.ds(3, count + 1, stride=4), :] = jnp.zeros((count + 1, nodes), f32)
    for copy in copies:
        copy.wait()
    for k in range(count // 2):
        rows = slice(8 * k, 8 * k + 8)
        left = jnp.concatenate([here[rows, :], prior[rows, :]], axis=1).astype(bf16)
        right = jnp.concatenate(
            [
                jnp.concatenate([stiff_ref[2 * k], stiff_ref[2 * k + 1]], axis=0),
                jnp.concatenate([coup_ref[2 * k], coup_ref[2 * k + 1]], axis=0),
            ],
            axis=1,
        )
        made[rows, :] = pick_half(nt_dot(left, right))
    for c in range(3):
        out_ref[c] = made[pl.ds(c, count, stride=4), :]


def residual(got_ref, kd_ref, inv_ref, disp_ref, diff_ref, base_ref, share_ref):
    count, nodes = disp_ref.shape[1:]
    peers = share_ref.shape[0]
    turned = got_ref[pl.ds(6, peers, stride=8), :].T
    block = iota((count, peers), 0).astype(f32)
    chosen = jnp.concatenate(
        [jnp.where(block == turned[i : i + 1, :], 1.0, 0.0) for i in range(2)], axis=1
    ).astype(bf16)
    res = []
    for c in range(3):
        rows = jnp.concatenate(
            [got_ref[pl.ds(c + 3 * i, peers, stride=8), :] for i in range(2)], axis=0
        )
        part = -inv_ref[c] * (kd_ref[c] - exact_dot(chosen, rows))
        base_ref[c] = disp_ref[c] + part
        res.append(part)
    columns = diff_ref.shape[0]
    sums = []
    for m in range(columns):
        part = sum(diff_ref[m, c] * res[c] for c in range(3))
        sums.append(jnp.sum(part, axis=0, keepdims=True))
    col = jnp.sum(jnp.concatenate(sums, axis=0), axis=1, keepdims=True)
    diag = iota((columns, nodes), 0) == iota((columns, nodes), 1)
    row = jnp.sum(jnp.where(diag, col, 0.0), axis=0, keepdims=True)
    share_ref[...] = jnp.broadcast_to(row, share_ref.shape)


def factor(blocks, got_ref, inverse_ref, serve_ref):
    spread, lanes = serve_ref.shape
    peers = spread // 8
    row = iota((8, lanes), 0)
    lane = iota((8, lanes), 1)
    second = row >= 3
    kept = ((lane // blocks) == jnp.where(second, row - 3, row)) & (row < 6)
    wanted = jnp.where(kept, lane % blocks, -2).astype(f32)
    for d in range(peers):
        tags = got_ref[8 * d + 6 : 8 * d + 7, :]
        tag = jnp.where(second, tags[:, 1:2], tags[:, 0:1])
        serve_ref[8 * d : 8 * d + 8, :] = jnp.where(tag == wanted, 1.0, 0.0).astype(bf16)
    total = jnp.sum(got_ref[pl.ds(7, peers, stride=8), :], axis=0, keepdims=True)
    n = 8
    gram = jnp.concatenate(
        [total if m == 0 else pltpu.roll(total, lanes - n * m, 1) for m in range(n)], axis=0
    )
    work = jnp.where(lane < n, gram, jnp.where(lane == row + n, 1.0, 0.0))
    for k in range(n):
        pivot = work[k : k + 1, :] * lax.rsqrt(work[k : k + 1, k : k + 1])
        below = work[:, k : k + 1] * lax.rsqrt(work[k : k + 1, k : k + 1])
        work = jnp.where(row == k, pivot, jnp.where(row > k, work - below * pivot, work))
    inverse_ref[...] = jnp.where(lane < n, pltpu.roll(work, lanes - n, 1), 0.0)


def update(share_ref, inverse_ref, base_ref, dd_ref, serve_ref, next_ref, reply_ref):
    projected = jnp.sum(share_ref[...], axis=0, keepdims=True)
    inverse = inverse_ref[...]
    middle = jnp.sum(inverse * projected, axis=1, keepdims=True)
    mixing = -jnp.sum(inverse * middle, axis=0, keepdims=True)
    rows = []
    for c in range(3):
        value = base_ref[c]
        for m in range(dd_ref.shape[0]):
            value = value + mixing[:, m : m + 1] * dd_ref[m, c]
        next_ref[c] = value
        rows.append(value)
    blocks = jnp.concatenate(rows, axis=0).astype(bf16)
    spare = serve_ref.shape[1] - blocks.shape[0]
    blocks = jnp.concatenate([blocks, jnp.zeros((spare, blocks.shape[1]), bf16)], axis=0)
    reply_ref[...] = jnp.dot(
        serve_ref[...], blocks, preferred_element_type=f32
    ).astype(bf16)


def motion(back_ref, slot_ref, rbf_ref, out_ref, picked, made):
    count = rbf_ref.shape[0]
    whole = (slot_ref.shape[0], back_ref.shape[0])
    pick = jnp.where(iota(whole, 1).astype(f32) == slot_ref[...], 1.0, 0.0).astype(bf16)
    picked[...] = jnp.dot(pick, back_ref[...], preferred_element_type=f32)
    for k in range(count // 2):
        rows = slice(8 * k, 8 * k + 8)
        both = jnp.concatenate([rbf_ref[2 * k], rbf_ref[2 * k + 1]], axis=0)
        made[rows, :] = pick_half(nt_dot(picked[rows, :].astype(bf16), both))
    for c in range(3):
        out_ref[c] = made[pl.ds(c, count, stride=4), :]


def exchange(value):
    return lax.all_to_all(value, AXES, split_axis=0, concat_axis=0, tiled=True)


def on_device(
    density, velocity, pressure, rbf, correlation, normals, routes, targets,
    stiffness, coupling, inverse_diag, displacement, diff_res, diff_disp,
):
    peers = lax.axis_size(AXES)
    depth, lanes = density.shape[1:]
    wide = -(-depth // 128) * 128
    count, nodes = correlation.shape
    blocks = displacement.shape[0]
    columns = diff_res.shape[0]
    normals, inverse_diag, displacement = (
        jnp.transpose(x, (1, 0, 2)) for x in (normals, inverse_diag, displacement)
    )
    diff_res, diff_disp = (jnp.transpose(x, (0, 2, 1, 3)) for x in (diff_res, diff_disp))
    ring = [(i, (i + 1) % peers) for i in range(peers)]
    back = [(j, i) for i, j in ring]

    own, second = call(
        edges,
        [shape((8, wide)), shape((8, wide))],
        density, velocity, pressure, displacement,
        fetched=(0, 1, 2, 3),
    )
    above = lax.ppermute(own, AXES, back)
    below = lax.ppermute(own, AXES, ring)
    scatter, slot, tag, gram, bulk, corr_near, normals_near, rbf_near = call(
        routing,
        [
            shape((8 * peers, 4 * count), bf16),
            shape((4 * count, 1)),
            shape((peers, nodes)),
            shape((1, nodes)),
            shape((5, depth, lanes), bf16),
            shape(correlation.shape, jnp.int32),
            shape(normals.shape),
            shape(rbf.shape, bf16),
        ],
        routes.reshape(1, count), targets.reshape(1, count), diff_res,
        density, velocity, pressure, correlation, normals, rbf,
        fetched=(0, 1, 2, 3, 4, 5),
        remote=(6, 7, 8),
        scratch=[pltpu.SemaphoreType.DMA((3,))],
    )
    bulk_below = lax.ppermute(bulk, AXES, ring)
    bulk_above = lax.ppermute(bulk, AXES, back)
    kernel = functools.partial(loads, depth)
    kernel.__name__ = "loads"
    sent = call(
        kernel,
        shape((8 * peers, nodes)),
        own, second, below, above, corr_near, normals_near, rbf_near, scatter, tag, gram,
        scratch=[pltpu.VMEM((4 * count, nodes), f32)] * 2,
    )
    got = exchange(sent.reshape(peers, 8, nodes)).reshape(8 * peers, nodes)
    keep = (lax.axis_index(AXES) > 0).astype(jnp.int32).reshape(1)
    product = call(
        solid,
        shape((3, blocks, nodes)),
        keep, displacement, below, stiffness, coupling,
        fetched=(3, 4),
        scalars=(0,),
        scratch=[
            pltpu.VMEM((4 * blocks, nodes), f32),
            pltpu.VMEM((4 * blocks + 8, nodes), f32),
            pltpu.VMEM((4 * blocks, nodes), f32),
        ],
    )
    base, share = call(
        residual,
        [shape((3, blocks, nodes)), shape((peers, nodes))],
        got, product, inverse_diag, displacement, diff_res,
    )
    shares = exchange(share)
    kernel = functools.partial(factor, blocks)
    kernel.__name__ = "factor"
    inverse, serve = call(
        kernel, [shape((columns, nodes)), shape((8 * peers, nodes), bf16)], got
    )
    disp_next, reply = call(
        update,
        [shape((3, blocks, nodes)), shape((8 * peers, nodes), bf16)],
        shares, inverse, base, diff_disp, serve,
    )
    returned = exchange(reply.reshape(peers, 8, nodes)).reshape(8 * peers, nodes)
    fluid_next = call(
        fluid,
        shape((5, 1, depth, lanes)),
        density, velocity, pressure, bulk_below, bulk_above,
        fetched=(0, 1, 2, 3, 4),
    )
    wall_motion = call(
        motion,
        shape((3, count, nodes)),
        returned, slot, rbf,
        scratch=[pltpu.VMEM((4 * count, nodes), f32)] * 2,
    )
    return (
        fluid_next,
        jnp.transpose(disp_next, (1, 0, 2)),
        jnp.transpose(wall_motion, (1, 0, 2)),
    )


def solution(mesh):
    rows = P(AXES, None, None)
    inner = P(None, AXES, None, None)
    return jax.shard_map(
        on_device,
        mesh=mesh,
        in_specs=(
            rows, inner, rows, rows, P(AXES, None), rows, P(AXES, None), P(AXES),
            rows, rows, rows, rows, inner, inner,
        ),
        out_specs=(inner, rows, rows),
        check_vma=False,
    )
```

```python
import functools

import jax
import jax.numpy as jnp
from jax import lax
from jax.experimental import pallas as pl
from jax.experimental.pallas import tpu as pltpu
from jax.sharding import PartitionSpec as P

AXES = ("group", "dev")
ratio_heat = 1.4
half_step = 0.5 * 0.03
f32 = jnp.float32
bf16 = jnp.bfloat16


def iota(shape, dim):
    return lax.broadcasted_iota(jnp.int32, shape, dim)


def call(kernel, out, *args, fetched=(), remote=(), scalars=(), scratch=(), limit=48):
    held = (*fetched, *remote)
    buffers = [pltpu.VMEM(args[i].shape, args[i].dtype) for i in fetched]
    if fetched:
        buffers.append(pltpu.SemaphoreType.DMA((len(fetched),)))
    args = [
        pltpu.with_memory_space_constraint(x, pltpu.HBM) if i in held else x
        for i, x in enumerate(args)
    ]
    return pl.pallas_call(
        kernel,
        out_shape=out,
        in_specs=[
            pl.BlockSpec(
                memory_space=pltpu.HBM
                if i in held
                else pltpu.SMEM
                if i in scalars
                else pltpu.VMEM
            )
            for i in range(len(args))
        ],
        scratch_shapes=buffers + list(scratch),
        compiler_params=pltpu.CompilerParams(vmem_limit_bytes=limit * 2**20),
        name=kernel.__name__,
    )(*args)


def fetch(sources, buffers, semaphores):
    copies = [
        pltpu.make_async_copy(source, buffer, semaphores.at[i])
        for i, (source, buffer) in enumerate(zip(sources, buffers))
    ]
    for copy in copies:
        copy.start()
    return copies


def shape(dims, dtype=f32):
    return jax.ShapeDtypeStruct(dims, dtype)


def conserve(cell):
    dens, v0, v1, v2, press = cell
    kinetic = v0 * v0 + v1 * v1 + v2 * v2
    energy = press * (1.0 / (ratio_heat - 1.0)) + 0.5 * dens * kinetic
    return (dens, dens * v0, dens * v1, dens * v2, energy)


def sound(cell):
    scaled = ratio_heat * cell[4]
    return scaled * lax.rsqrt(scaled * cell[0])


def with_speed(cell):
    return (cell, conserve(cell), sound(cell))


def euler_flux(state, axis):
    cell, cons, speed = state
    normal = cell[1 + axis]
    rows = [cons[1 + axis]]
    for comp in range(3):
        moment = cons[1 + comp] * normal
        rows.append(moment + cell[4] if comp == axis else moment)
    rows.append((cons[4] + cell[4]) * normal)
    return rows, jnp.abs(normal) + speed


def rusanov(left, right, axis):
    flux_left, speed_left = euler_flux(left, axis)
    flux_right, speed_right = euler_flux(right, axis)
    top = jnp.maximum(speed_left, speed_right)
    return [
        a + b - top * (r - l)
        for a, b, l, r in zip(flux_left, flux_right, left[1], right[1])
    ]


def divergence(left, me, right, axis):
    flux_left, speed_left = euler_flux(left, axis)
    flux_right, speed_right = euler_flux(right, axis)
    own = jnp.abs(me[0][1 + axis]) + me[2]
    low, high = jnp.maximum(speed_left, own), jnp.maximum(own, speed_right)
    return [
        b - a - high * (r - c) + low * (c - l)
        for a, b, l, c, r in zip(flux_left, flux_right, left[1], me[1], right[1])
    ]


def wall_flux(state):
    cell, cons, speed = state
    return 2.0 * (cons[3] * cell[3] + cell[4] - (jnp.abs(cell[3]) + speed) * cons[3])


def edges(
    dens_hbm, vel_hbm, press_hbm, disp_hbm, send_ref, second_ref,
    dens_ref, vel_ref, press_ref, disp_ref, semaphores,
):
    copies = fetch(
        (dens_hbm, vel_hbm, press_hbm, disp_hbm),
        (dens_ref, vel_ref, press_ref, disp_ref),
        semaphores,
    )
    depth, lanes = dens_ref.shape[1:]
    wide = send_ref.shape[1]
    lane = iota((depth, lanes), 1)
    packed = jnp.ones((depth, lanes), f32)
    rows = [
        (copies[0], dens_ref.at[0]),
        (copies[1], vel_ref.at[0, 0]),
        (None, vel_ref.at[1, 0]),
        (None, vel_ref.at[2, 0]),
        (copies[2], press_ref.at[0]),
    ]
    for i, (copy, ref) in enumerate(rows):
        if copy is not None:
            copy.wait()
        row = ref[...]
        moved = row if i == 0 else pltpu.roll(row, 2 * i, 1)
        packed = jnp.where((lane >> 1) == i, moved, packed)
    packed = jnp.concatenate([packed, jnp.ones((wide - depth, lanes), f32)], axis=0)
    turned = packed.T
    last = disp_ref.shape[1] - 1
    copies[3].wait()
    for i in range(5):
        send_ref[i : i + 1, :] = turned[2 * i : 2 * i + 1, :]
        second_ref[i : i + 1, :] = turned[2 * i + 1 : 2 * i + 2, :]
    nodes = disp_ref.shape[2]
    for c in range(3):
        send_ref[5:6, c * nodes : (c + 1) * nodes] = disp_ref[c, last : last + 1, :]
    send_ref[6:8, :] = jnp.zeros((2, wide), f32)
    second_ref[5:8, :] = jnp.zeros((3, wide), f32)


def fluid(
    dens_hbm, vel_hbm, press_hbm, below_hbm, above_hbm, next_ref,
    dens_ref, vel_ref, press_ref, below_ref, above_ref, semaphores,
):
    for copy in fetch(
        (dens_hbm, vel_hbm, press_hbm, below_hbm, above_hbm),
        (dens_ref, vel_ref, press_ref, below_ref, above_ref),
        semaphores,
    ):
        copy.wait()
    depth, lanes = dens_ref.shape[1:]
    rows = 16
    sub = iota((rows, lanes), 0)
    lane = iota((rows, lanes), 1)

    def load(at):
        return (
            dens_ref[0, at, :],
            vel_ref[0, 0, at, :],
            vel_ref[1, 0, at, :],
            vel_ref[2, 0, at, :],
            press_ref[0, at, :],
        )

    def step(i, carried):
        start = pl.multiple_of(i * rows, rows)
        after = pl.multiple_of(jnp.where(start + rows == depth, 0, start + rows), 8)
        at = pl.ds(start, rows)
        cell = load(at)
        ahead = load(pl.ds(after, 8))
        me = with_speed(cell)
        below = with_speed([below_ref[q, at, :].astype(f32) for q in range(5)])
        above = with_speed([above_ref[q, at, :].astype(f32) for q in range(5)])
        total = divergence(below, me, above, 0)
        beside = with_speed(
            [
                jnp.where(sub == rows - 1, n[0:1, :], pltpu.roll(x, rows - 1, 0))
                for x, n in zip(cell, ahead)
            ]
        )
        face = rusanov(me, beside, 1)
        total = [
            t + f - jnp.where(sub == 0, c, pltpu.roll(f, 1, 0))
            for t, f, c in zip(total, face, carried)
        ]
        carried = tuple(f[rows - 1 : rows, :] for f in face)
        over = with_speed(
            [jnp.where(lane == lanes - 1, x, pltpu.roll(x, lanes - 1, 1)) for x in cell]
        )
        face = rusanov(me, over, 2)
        wall = wall_flux(me)
        for q in range(5):
            lower = jnp.where(
                lane == 0, wall if q == 3 else 0.0, pltpu.roll(face[q], 1, 1)
            )
            next_ref[q, 0, at, :] = me[1][q] - half_step * (total[q] + face[q] - lower)
        return carried

    first = with_speed([x[0:1, :] for x in load(pl.ds(0, 8))])
    last = with_speed([x[7:8, :] for x in load(pl.ds(depth - 8, 8))])
    lax.fori_loop(0, depth // rows, step, tuple(rusanov(last, first, 1)))


def row_cell(ref):
    return [ref[i : i + 1, :] for i in range(5)]


def wall_start(depth, own, second):
    wide = own[0].shape[1]
    lane = iota((1, wide), 1)
    me = with_speed(own)

    def up(x):
        return jnp.where(lane == depth - 1, x[:, 0:1], pltpu.roll(x, wide - 1, 1))

    def down(x):
        return jnp.where(lane == 0, x[:, depth - 1 : depth], pltpu.roll(x, 1, 1))

    face = rusanov(me, with_speed([up(x) for x in own]), 1)
    total = [f - down(f) for f in face]
    face = rusanov(me, with_speed(second), 2)
    total = [t + f for t, f in zip(total, face)]
    total[3] = total[3] - wall_flux(me)
    return [c - half_step * t for c, t in zip(me[1], total)]


def wall_pressure(start, own, below, above):
    total = divergence(with_speed(below), with_speed(own), with_speed(above), 0)
    q = [c - half_step * t for c, t in zip(start, total)]
    return (ratio_heat - 1.0) * (
        q[4] - 0.5 * (q[1] * q[1] + q[2] * q[2] + q[3] * q[3]) / q[0]
    )


def routing(
    groups, routes_hbm, targets_hbm, diff_hbm, dens_hbm, vel_hbm, press_hbm,
    corr_hbm, normals_hbm, rbf_hbm, own_ref, second_ref,
    start_ref, scatter_ref, slot_ref, tag_ref, gram_ref, bulk_ref, corr_ref, normals_ref, rbf_ref,
    routes_ref, targets_ref, diff_ref, dens_ref, vel_ref, press_ref, semaphores, ahead,
):
    copies = fetch(
        (routes_hbm, targets_hbm, diff_hbm, dens_hbm, vel_hbm, press_hbm),
        (routes_ref, targets_ref, diff_ref, dens_ref, vel_ref, press_ref),
        semaphores,
    )
    later = fetch((corr_hbm, normals_hbm, rbf_hbm), (corr_ref, normals_ref, rbf_ref), ahead)
    start = wall_start(dens_ref.shape[1], row_cell(own_ref), row_cell(second_ref))
    for i in range(5):
        start_ref[i : i + 1, :] = start[i]
    start_ref[5:8, :] = jnp.zeros((3, start_ref.shape[1]), f32)
    copies[0].wait()
    copies[1].wait()
    count = routes_ref.shape[1]
    spread, taken = scatter_ref.shape
    peers = tag_ref.shape[0]
    ii, jj = iota((count, count), 0), iota((count, count), 1)
    inner = peers // groups
    routes = routes_ref[...]
    routes = (routes & (inner - 1)) * groups + (routes >> (inner.bit_length() - 1))
    route_row = jnp.broadcast_to(routes, (count, count)).astype(f32)
    target_row = jnp.broadcast_to(targets_ref[...], (count, count)).astype(f32)
    route_col = jnp.sum(jnp.where(ii == jj, route_row, 0.0), axis=1, keepdims=True)
    target_col = jnp.sum(jnp.where(ii == jj, target_row, 0.0), axis=1, keepdims=True)
    same = jnp.where(route_col == route_row, 1.0, 0.0)
    place_col = jnp.sum(jnp.where(jj < ii, same, 0.0), axis=1, keepdims=True)
    place_row = jnp.sum(jnp.where(ii < jj, same, 0.0), axis=0, keepdims=True)
    slot_col = route_col * 8.0 + place_col * 3.0
    slot_row = route_row[0:1, :] * 8.0 + place_row * 3.0
    own = (iota((count, taken), 1) >> 2) == iota((count, taken), 0)
    comp = iota((1, taken), 1) & 3
    at_row = jnp.sum(jnp.where(own, slot_col, 0.0), axis=0, keepdims=True)
    at_row = jnp.where(comp < 3, at_row + comp.astype(f32), -1.0)
    scatter_ref[...] = jnp.where(
        iota((spread, taken), 0).astype(f32) == at_row, 1.0, 0.0
    ).astype(bf16)
    own = (iota((taken, count), 0) >> 2) == iota((taken, count), 1)
    comp = iota((taken, 1), 0) & 3
    at_col = jnp.sum(jnp.where(own, slot_row, 0.0), axis=1, keepdims=True)
    at_col = jnp.where(comp < 3, at_col + comp.astype(f32), -1.0)
    slot_ref[...] = at_col
    to_peer = jnp.where(
        iota((peers, count), 0).astype(f32) == route_row[0:1, :], 1.0, 0.0
    )
    named = jnp.where(
        iota((count, tag_ref.shape[1]), 1).astype(f32) == place_col, target_col + 1.0, 0.0
    )
    tag_ref[...] = (
        jnp.dot(to_peer.astype(bf16), named.astype(bf16), preferred_element_type=f32) - 1.0
    )
    copies[2].wait()
    columns = diff_ref.shape[0]
    lanes = diff_ref.shape[3]
    sums = {}
    for m in range(columns):
        for n in range(m, columns):
            part = jnp.sum(diff_ref[m] * diff_ref[n], axis=0)
            sums[m, n] = jnp.sum(part, axis=0, keepdims=True)
    stacked = jnp.concatenate(
        [sums[min(m, n), max(m, n)] for m in range(columns) for n in range(columns)], axis=0
    )
    col = jnp.sum(stacked, axis=1, keepdims=True)
    diag = iota((columns * columns, lanes), 0) == iota((columns * columns, lanes), 1)
    gram_ref[...] = jnp.sum(jnp.where(diag, col, 0.0), axis=0, keepdims=True)
    for copy in copies[3:] + later:
        copy.wait()
    bulk_ref[0] = dens_ref[0].astype(bf16)
    for c in range(3):
        bulk_ref[1 + c] = vel_ref[c, 0].astype(bf16)
    bulk_ref[4] = press_ref[0].astype(bf16)


def thirds(value):
    high = value.astype(bf16)
    rest = value - high.astype(f32)
    middle = rest.astype(bf16)
    return high, middle, (rest - middle.astype(f32)).astype(bf16)


def exact_dot(onehot, value):
    parts = jnp.concatenate(thirds(value), axis=1)
    made = jnp.dot(onehot, parts, preferred_element_type=f32)
    lanes = value.shape[1]
    return made[:, :lanes] + made[:, lanes : 2 * lanes] + made[:, 2 * lanes :]


def pick_half(both):
    lanes = both.shape[1] // 2
    return jnp.where(iota((8, lanes), 0) < 4, both[:, :lanes], both[:, lanes:])


def nt_dot(a, b):
    return lax.dot_general(a, b, (((1,), (1,)), ((), ())), preferred_element_type=f32)


def loads(
    start_ref, own_ref, below_ref, above_ref, corr_ref, normals_ref, rbf_ref,
    scatter_ref, tag_ref, gram_ref, send_ref, weighted, mapped,
):
    wall = wall_pressure(
        row_cell(start_ref), row_cell(own_ref), row_cell(below_ref), row_cell(above_ref)
    )
    count, nodes = corr_ref.shape
    at = corr_ref[...]
    within, part = at & (nodes - 1), at >> (nodes.bit_length() - 1)
    found = jnp.zeros((count, nodes), f32)
    for k in range(wall.shape[1] // nodes):
        table = jnp.broadcast_to(wall[:, k * nodes : (k + 1) * nodes], (count, nodes))
        got = jnp.take_along_axis(table, within, axis=1, mode="promise_in_bounds")
        found = jnp.where(part == k, got, found)
    for c in range(3):
        weighted[pl.ds(c, count, stride=4), :] = found * normals_ref[c]
    weighted[pl.ds(3, count, stride=4), :] = jnp.zeros((count, nodes), f32)
    for k in range(count // 2):
        both = jnp.concatenate([rbf_ref[2 * k], rbf_ref[2 * k + 1]], axis=1)
        left = weighted[8 * k : 8 * k + 8, :].astype(bf16)
        mapped[8 * k : 8 * k + 8, :] = pick_half(
            jnp.dot(left, both, preferred_element_type=f32)
        )
    send_ref[...] = exact_dot(scatter_ref[...], mapped[...])
    peers = tag_ref.shape[0]
    send_ref[pl.ds(6, peers, stride=8), :] = tag_ref[...]
    send_ref[pl.ds(7, peers, stride=8), :] = jnp.broadcast_to(gram_ref[...], tag_ref.shape)


def solid(
    keep_ref, disp_ref, below_ref, stiff_hbm, coup_hbm, out_ref,
    stiff_ref, coup_ref, semaphores, here, prior, made,
):
    copies = fetch((stiff_hbm, coup_hbm), (stiff_ref, coup_ref), semaphores)
    count, nodes = disp_ref.shape[1:]
    for c in range(3):
        here[pl.ds(c, count, stride=4), :] = disp_ref[c]
        prior[pl.ds(4 + c, count, stride=4), :] = disp_ref[c]
        first = below_ref[5:6, c * nodes : (c + 1) * nodes]
        prior[c : c + 1, :] = jnp.where(keep_ref[0] > 0, first, 0.0)
    here[pl.ds(3, count, stride=4), :] = jnp.zeros((count, nodes), f32)
    prior[pl.ds(3, count + 1, stride=4), :] = jnp.zeros((count + 1, nodes), f32)
    for copy in copies:
        copy.wait()
    for k in range(count // 2):
        rows = slice(8 * k, 8 * k + 8)
        left = jnp.concatenate([here[rows, :], prior[rows, :]], axis=1).astype(bf16)
        right = jnp.concatenate(
            [
                jnp.concatenate([stiff_ref[2 * k], stiff_ref[2 * k + 1]], axis=0),
                jnp.concatenate([coup_ref[2 * k], coup_ref[2 * k + 1]], axis=0),
            ],
            axis=1,
        )
        made[rows, :] = pick_half(nt_dot(left, right))
    for c in range(3):
        out_ref[c] = made[pl.ds(c, count, stride=4), :]


def residual(got_ref, kd_ref, inv_ref, disp_ref, diff_ref, base_ref, share_ref):
    count, nodes = disp_ref.shape[1:]
    peers = share_ref.shape[0]
    turned = got_ref[pl.ds(6, peers, stride=8), :].T
    block = iota((count, peers), 0).astype(f32)
    chosen = jnp.concatenate(
        [jnp.where(block == turned[i : i + 1, :], 1.0, 0.0) for i in range(2)], axis=1
    ).astype(bf16)
    res = []
    for c in range(3):
        rows = jnp.concatenate(
            [got_ref[pl.ds(c + 3 * i, peers, stride=8), :] for i in range(2)], axis=0
        )
        part = -inv_ref[c] * (kd_ref[c] - exact_dot(chosen, rows))
        base_ref[c] = disp_ref[c] + part
        res.append(part)
    columns = diff_ref.shape[0]
    sums = []
    for m in range(columns):
        part = sum(diff_ref[m, c] * res[c] for c in range(3))
        sums.append(jnp.sum(part, axis=0, keepdims=True))
    col = jnp.sum(jnp.concatenate(sums, axis=0), axis=1, keepdims=True)
    diag = iota((columns, nodes), 0) == iota((columns, nodes), 1)
    row = jnp.sum(jnp.where(diag, col, 0.0), axis=0, keepdims=True)
    share_ref[...] = jnp.broadcast_to(row, share_ref.shape)


def factor(
    blocks, got_ref, dd_hbm, inverse_ref, serve_ref, turned_ref, dd_ref, semaphores
):
    copies = fetch((dd_hbm,), (dd_ref,), semaphores)
    spread, lanes = serve_ref.shape
    peers = spread // 8
    row = iota((8, lanes), 0)
    lane = iota((8, lanes), 1)
    second = row >= 3
    kept = ((lane // blocks) == jnp.where(second, row - 3, row)) & (row < 6)
    wanted = jnp.where(kept, lane % blocks, -2).astype(f32)
    for d in range(peers):
        tags = got_ref[8 * d + 6 : 8 * d + 7, :]
        tag = jnp.where(second, tags[:, 1:2], tags[:, 0:1])
        serve_ref[8 * d : 8 * d + 8, :] = jnp.where(tag == wanted, 1.0, 0.0).astype(bf16)
    total = jnp.sum(got_ref[pl.ds(7, peers, stride=8), :], axis=0, keepdims=True)
    n = 8
    gram = jnp.concatenate(
        [total if m == 0 else pltpu.roll(total, lanes - n * m, 1) for m in range(n)], axis=0
    )
    work = jnp.where(lane < n, gram, jnp.where(lane == row + n, 1.0, 0.0))
    for k in range(n):
        pivot = work[k : k + 1, :] * lax.rsqrt(work[k : k + 1, k : k + 1])
        below = work[:, k : k + 1] * lax.rsqrt(work[k : k + 1, k : k + 1])
        work = jnp.where(row == k, pivot, jnp.where(row > k, work - below * pivot, work))
    inverse = jnp.where(lane < n, pltpu.roll(work, lanes - n, 1), 0.0)
    inverse_ref[...] = inverse
    copies[0].wait()
    for k in range(n):
        for c in range(3):
            turned_ref[k, c] = sum(
                inverse[k : k + 1, m : m + 1] * dd_ref[m, c] for m in range(k + 1)
            )


def update(share_ref, inverse_ref, base_ref, turned_ref, serve_ref, next_ref, reply_ref):
    projected = jnp.sum(share_ref[...], axis=0, keepdims=True)
    middle = jnp.sum(inverse_ref[...] * projected, axis=1, keepdims=True)
    rows = []
    for c in range(3):
        value = base_ref[c]
        for k in range(turned_ref.shape[0]):
            value = value - middle[k : k + 1, :] * turned_ref[k, c]
        next_ref[c] = value
        rows.append(value)
    blocks = jnp.concatenate(rows, axis=0).astype(bf16)
    spare = serve_ref.shape[1] - blocks.shape[0]
    blocks = jnp.concatenate([blocks, jnp.zeros((spare, blocks.shape[1]), bf16)], axis=0)
    reply_ref[...] = jnp.dot(
        serve_ref[...], blocks, preferred_element_type=f32
    ).astype(bf16)


def prepare(slot_ref, rbf_hbm, pick_ref, turned_ref, rbf_ref, semaphores):
    copies = fetch((rbf_hbm,), (rbf_ref,), semaphores)
    wanted = iota(pick_ref.shape, 1).astype(f32) == slot_ref[...]
    pick_ref[...] = jnp.where(wanted, 1.0, 0.0).astype(bf16)
    copies[0].wait()
    for b in range(rbf_ref.shape[0]):
        turned_ref[b] = rbf_ref[b].T


def motion(back_ref, pick_ref, turned_ref, out_ref, picked, made):
    count = turned_ref.shape[0]
    picked[...] = jnp.dot(pick_ref[...], back_ref[...], preferred_element_type=f32)
    for k in range(count // 2):
        rows = slice(8 * k, 8 * k + 8)
        both = jnp.concatenate([turned_ref[2 * k], turned_ref[2 * k + 1]], axis=1)
        left = picked[rows, :].astype(bf16)
        made[rows, :] = pick_half(jnp.dot(left, both, preferred_element_type=f32))
    for c in range(3):
        out_ref[c] = made[pl.ds(c, count, stride=4), :]


def exchange(value):
    return lax.all_to_all(value, AXES[::-1], split_axis=0, concat_axis=0, tiled=True)


def on_device(
    density, velocity, pressure, rbf, correlation, normals, routes, targets,
    stiffness, coupling, inverse_diag, displacement, diff_res, diff_disp,
):
    peers = lax.axis_size(AXES)
    depth, lanes = density.shape[1:]
    wide = -(-depth // 128) * 128
    count, nodes = correlation.shape
    blocks = displacement.shape[0]
    columns = diff_res.shape[0]
    normals, inverse_diag, displacement = (
        jnp.transpose(x, (1, 0, 2)) for x in (normals, inverse_diag, displacement)
    )
    diff_res, diff_disp = (jnp.transpose(x, (0, 2, 1, 3)) for x in (diff_res, diff_disp))
    ring = [(i, (i + 1) % peers) for i in range(peers)]
    back = [(j, i) for i, j in ring]

    own, second = call(
        edges,
        [shape((8, wide)), shape((8, wide))],
        density, velocity, pressure, displacement,
        fetched=(0, 1, 2, 3),
    )
    above = lax.ppermute(own, AXES, back)
    below = lax.ppermute(own, AXES, ring)
    kernel = functools.partial(routing, lax.axis_size(AXES[0]))
    kernel.__name__ = "routing"
    start, scatter, slot, tag, gram, bulk, corr_near, normals_near, rbf_near = call(
        kernel,
        [
            shape((8, wide)),
            shape((8 * peers, 4 * count), bf16),
            shape((4 * count, 1)),
            shape((peers, nodes)),
            shape((1, nodes)),
            shape((5, depth, lanes), bf16),
            shape(correlation.shape, jnp.int32),
            shape(normals.shape),
            shape(rbf.shape, bf16),
        ],
        routes.reshape(1, count), targets.reshape(1, count), diff_res,
        density, velocity, pressure, correlation, normals, rbf, own, second,
        fetched=(0, 1, 2, 3, 4, 5),
        remote=(6, 7, 8),
        scratch=[pltpu.SemaphoreType.DMA((3,))],
    )
    bulk_below = lax.ppermute(bulk, AXES, ring)
    bulk_above = lax.ppermute(bulk, AXES, back)
    sent = call(
        loads,
        shape((8 * peers, nodes)),
        start, own, below, above, corr_near, normals_near, rbf_near, scatter, tag, gram,
        scratch=[pltpu.VMEM((4 * count, nodes), f32)] * 2,
    )
    got = exchange(sent.reshape(peers, 8, nodes)).reshape(8 * peers, nodes)
    keep = (lax.axis_index(AXES) > 0).astype(jnp.int32).reshape(1)
    product = call(
        solid,
        shape((3, blocks, nodes)),
        keep, displacement, below, stiffness, coupling,
        fetched=(3, 4),
        scalars=(0,),
        scratch=[
            pltpu.VMEM((4 * blocks, nodes), f32),
            pltpu.VMEM((4 * blocks + 8, nodes), f32),
            pltpu.VMEM((4 * blocks, nodes), f32),
        ],
    )
    base, share = call(
        residual,
        [shape((3, blocks, nodes)), shape((peers, nodes))],
        got, product, inverse_diag, displacement, diff_res,
    )
    shares = exchange(share)
    kernel = functools.partial(factor, blocks)
    kernel.__name__ = "factor"
    inverse, serve, turned = call(
        kernel,
        [
            shape((columns, nodes)),
            shape((8 * peers, nodes), bf16),
            shape((columns, 3, blocks, nodes)),
        ],
        got, diff_disp,
        fetched=(1,),
    )
    disp_next, reply = call(
        update,
        [shape((3, blocks, nodes)), shape((8 * peers, nodes), bf16)],
        shares, inverse, base, turned, serve,
    )
    returned = exchange(reply.reshape(peers, 8, nodes)).reshape(8 * peers, nodes)
    fluid_next = call(
        fluid,
        shape((5, 1, depth, lanes)),
        density, velocity, pressure, bulk_below, bulk_above,
        fetched=(0, 1, 2, 3, 4),
    )
    pick, rbf_turned = call(
        prepare,
        [shape((4 * count, 8 * peers), bf16), shape(rbf.shape, bf16)],
        slot, rbf,
        fetched=(1,),
    )
    wall_motion = call(
        motion,
        shape((3, count, nodes)),
        returned, pick, rbf_turned,
        scratch=[pltpu.VMEM((4 * count, nodes), f32)] * 2,
    )
    return (
        fluid_next,
        jnp.transpose(disp_next, (1, 0, 2)),
        jnp.transpose(wall_motion, (1, 0, 2)),
    )


def solution(mesh):
    rows = P(AXES, None, None)
    inner = P(None, AXES, None, None)
    return jax.shard_map(
        on_device,
        mesh=mesh,
        in_specs=(
            rows, inner, rows, rows, P(AXES, None), rows, P(AXES, None), P(AXES),
            rows, rows, rows, rows, inner, inner,
        ),
        out_specs=(inner, rows, rows),
        check_vma=False,
    )
```

```python
import functools

import jax
import jax.numpy as jnp
from jax import lax
from jax.experimental import pallas as pl
from jax.experimental.pallas import tpu as pltpu
from jax.sharding import PartitionSpec as P

AXES = ("group", "dev")
ratio_heat = 1.4
half_step = 0.5 * 0.03
f32 = jnp.float32
bf16 = jnp.bfloat16


def iota(shape, dim):
    return lax.broadcasted_iota(jnp.int32, shape, dim)


def call(kernel, out, *args, fetched=(), remote=(), scalars=(), scratch=(), limit=48):
    held = (*fetched, *remote)
    buffers = [pltpu.VMEM(args[i].shape, args[i].dtype) for i in fetched]
    if fetched:
        buffers.append(pltpu.SemaphoreType.DMA((len(fetched),)))
    args = [
        pltpu.with_memory_space_constraint(x, pltpu.HBM) if i in held else x
        for i, x in enumerate(args)
    ]
    return pl.pallas_call(
        kernel,
        out_shape=out,
        in_specs=[
            pl.BlockSpec(
                memory_space=pltpu.HBM
                if i in held
                else pltpu.SMEM
                if i in scalars
                else pltpu.VMEM
            )
            for i in range(len(args))
        ],
        scratch_shapes=buffers + list(scratch),
        compiler_params=pltpu.CompilerParams(vmem_limit_bytes=limit * 2**20),
        name=kernel.__name__,
    )(*args)


def fetch(sources, buffers, semaphores):
    copies = [
        pltpu.make_async_copy(source, buffer, semaphores.at[i])
        for i, (source, buffer) in enumerate(zip(sources, buffers))
    ]
    for copy in copies:
        copy.start()
    return copies


def shape(dims, dtype=f32):
    return jax.ShapeDtypeStruct(dims, dtype)


def conserve(cell):
    dens, v0, v1, v2, press = cell
    kinetic = v0 * v0 + v1 * v1 + v2 * v2
    energy = press * (1.0 / (ratio_heat - 1.0)) + 0.5 * dens * kinetic
    return (dens, dens * v0, dens * v1, dens * v2, energy)


def sound(cell):
    scaled = ratio_heat * cell[4]
    return scaled * lax.rsqrt(scaled * cell[0])


def with_speed(cell):
    return (cell, conserve(cell), sound(cell))


def euler_flux(state, axis):
    cell, cons, speed = state
    normal = cell[1 + axis]
    rows = [cons[1 + axis]]
    for comp in range(3):
        moment = cons[1 + comp] * normal
        rows.append(moment + cell[4] if comp == axis else moment)
    rows.append((cons[4] + cell[4]) * normal)
    return rows, jnp.abs(normal) + speed


def rusanov(left, right, axis):
    flux_left, speed_left = euler_flux(left, axis)
    flux_right, speed_right = euler_flux(right, axis)
    top = jnp.maximum(speed_left, speed_right)
    return [
        a + b - top * (r - l)
        for a, b, l, r in zip(flux_left, flux_right, left[1], right[1])
    ]


def divergence(left, me, right, axis):
    flux_left, speed_left = euler_flux(left, axis)
    flux_right, speed_right = euler_flux(right, axis)
    own = jnp.abs(me[0][1 + axis]) + me[2]
    low, high = jnp.maximum(speed_left, own), jnp.maximum(own, speed_right)
    return [
        b - a - high * (r - c) + low * (c - l)
        for a, b, l, c, r in zip(flux_left, flux_right, left[1], me[1], right[1])
    ]


def wall_flux(state):
    cell, cons, speed = state
    return 2.0 * (cons[3] * cell[3] + cell[4] - (jnp.abs(cell[3]) + speed) * cons[3])


def edges(
    dens_hbm, vel_hbm, press_hbm, disp_hbm, send_ref, second_ref,
    dens_ref, vel_ref, press_ref, disp_ref, semaphores,
):
    copies = fetch(
        (dens_hbm, vel_hbm, press_hbm, disp_hbm),
        (dens_ref, vel_ref, press_ref, disp_ref),
        semaphores,
    )
    depth, lanes = dens_ref.shape[1:]
    wide = send_ref.shape[1]
    lane = iota((depth, lanes), 1)
    packed = jnp.ones((depth, lanes), f32)
    rows = [
        (copies[0], dens_ref.at[0]),
        (copies[1], vel_ref.at[0, 0]),
        (None, vel_ref.at[1, 0]),
        (None, vel_ref.at[2, 0]),
        (copies[2], press_ref.at[0]),
    ]
    for i, (copy, ref) in enumerate(rows):
        if copy is not None:
            copy.wait()
        row = ref[...]
        moved = row if i == 0 else pltpu.roll(row, 2 * i, 1)
        packed = jnp.where((lane >> 1) == i, moved, packed)
    packed = jnp.concatenate([packed, jnp.ones((wide - depth, lanes), f32)], axis=0)
    turned = packed.T
    last = disp_ref.shape[1] - 1
    copies[3].wait()
    for i in range(5):
        send_ref[i : i + 1, :] = turned[2 * i : 2 * i + 1, :]
        second_ref[i : i + 1, :] = turned[2 * i + 1 : 2 * i + 2, :]
    nodes = disp_ref.shape[2]
    for c in range(3):
        send_ref[5:6, c * nodes : (c + 1) * nodes] = disp_ref[c, last : last + 1, :]
    send_ref[6:8, :] = jnp.zeros((2, wide), f32)
    second_ref[5:8, :] = jnp.zeros((3, wide), f32)


def fluid(
    dens_hbm, vel_hbm, press_hbm, below_hbm, above_hbm, next_ref,
    dens_ref, vel_ref, press_ref, below_ref, above_ref, semaphores,
):
    for copy in fetch(
        (dens_hbm, vel_hbm, press_hbm, below_hbm, above_hbm),
        (dens_ref, vel_ref, press_ref, below_ref, above_ref),
        semaphores,
    ):
        copy.wait()
    depth, lanes = dens_ref.shape[1:]
    rows = 16
    sub = iota((rows, lanes), 0)
    lane = iota((rows, lanes), 1)

    def load(at):
        return (
            dens_ref[0, at, :],
            vel_ref[0, 0, at, :],
            vel_ref[1, 0, at, :],
            vel_ref[2, 0, at, :],
            press_ref[0, at, :],
        )

    def step(i, carried):
        start = pl.multiple_of(i * rows, rows)
        after = pl.multiple_of(jnp.where(start + rows == depth, 0, start + rows), 8)
        at = pl.ds(start, rows)
        cell = load(at)
        ahead = load(pl.ds(after, 8))
        me = with_speed(cell)
        below = with_speed([below_ref[q, at, :].astype(f32) for q in range(5)])
        above = with_speed([above_ref[q, at, :].astype(f32) for q in range(5)])
        total = divergence(below, me, above, 0)
        beside = with_speed(
            [
                jnp.where(sub == rows - 1, n[0:1, :], pltpu.roll(x, rows - 1, 0))
                for x, n in zip(cell, ahead)
            ]
        )
        face = rusanov(me, beside, 1)
        total = [
            t + f - jnp.where(sub == 0, c, pltpu.roll(f, 1, 0))
            for t, f, c in zip(total, face, carried)
        ]
        carried = tuple(f[rows - 1 : rows, :] for f in face)
        over = with_speed(
            [jnp.where(lane == lanes - 1, x, pltpu.roll(x, lanes - 1, 1)) for x in cell]
        )
        face = rusanov(me, over, 2)
        wall = wall_flux(me)
        for q in range(5):
            lower = jnp.where(
                lane == 0, wall if q == 3 else 0.0, pltpu.roll(face[q], 1, 1)
            )
            next_ref[q, 0, at, :] = me[1][q] - half_step * (total[q] + face[q] - lower)
        return carried

    first = with_speed([x[0:1, :] for x in load(pl.ds(0, 8))])
    last = with_speed([x[7:8, :] for x in load(pl.ds(depth - 8, 8))])
    lax.fori_loop(0, depth // rows, step, tuple(rusanov(last, first, 1)))


def row_cell(ref):
    return [ref[i : i + 1, :] for i in range(5)]


def wall_start(depth, own, second):
    wide = own[0].shape[1]
    lane = iota((1, wide), 1)
    me = with_speed(own)

    def up(x):
        return jnp.where(lane == depth - 1, x[:, 0:1], pltpu.roll(x, wide - 1, 1))

    def down(x):
        return jnp.where(lane == 0, x[:, depth - 1 : depth], pltpu.roll(x, 1, 1))

    face = rusanov(me, with_speed([up(x) for x in own]), 1)
    total = [f - down(f) for f in face]
    face = rusanov(me, with_speed(second), 2)
    total = [t + f for t, f in zip(total, face)]
    total[3] = total[3] - wall_flux(me)
    return [c - half_step * t for c, t in zip(me[1], total)]


def wall_pressure(start, own, below, above):
    total = divergence(with_speed(below), with_speed(own), with_speed(above), 0)
    q = [c - half_step * t for c, t in zip(start, total)]
    return (ratio_heat - 1.0) * (
        q[4] - 0.5 * (q[1] * q[1] + q[2] * q[2] + q[3] * q[3]) / q[0]
    )


sent_rows = 7
reply_rows = 6
gram_lane = 64


def routing(
    groups, routes_hbm, targets_hbm, diff_hbm, dens_hbm, vel_hbm, press_hbm,
    corr_hbm, normals_hbm, rbf_hbm, own_ref, second_ref,
    start_ref, scatter_ref, slot_ref, meta_ref, bulk_ref, corr_ref, normals_ref, rbf_ref,
    routes_ref, targets_ref, diff_ref, dens_ref, vel_ref, press_ref, semaphores, ahead,
):
    copies = fetch(
        (routes_hbm, targets_hbm, diff_hbm, dens_hbm, vel_hbm, press_hbm),
        (routes_ref, targets_ref, diff_ref, dens_ref, vel_ref, press_ref),
        semaphores,
    )
    later = fetch((corr_hbm, normals_hbm, rbf_hbm), (corr_ref, normals_ref, rbf_ref), ahead)
    start = wall_start(dens_ref.shape[1], row_cell(own_ref), row_cell(second_ref))
    for i in range(5):
        start_ref[i : i + 1, :] = start[i]
    start_ref[5:8, :] = jnp.zeros((3, start_ref.shape[1]), f32)
    copies[0].wait()
    copies[1].wait()
    count = routes_ref.shape[1]
    spread, taken = scatter_ref.shape
    peers = meta_ref.shape[0]
    ii, jj = iota((count, count), 0), iota((count, count), 1)
    inner = peers // groups
    routes = routes_ref[...]
    routes = (routes & (inner - 1)) * groups + (routes >> (inner.bit_length() - 1))
    route_row = jnp.broadcast_to(routes, (count, count)).astype(f32)
    target_row = jnp.broadcast_to(targets_ref[...], (count, count)).astype(f32)
    route_col = jnp.sum(jnp.where(ii == jj, route_row, 0.0), axis=1, keepdims=True)
    target_col = jnp.sum(jnp.where(ii == jj, target_row, 0.0), axis=1, keepdims=True)
    same = jnp.where(route_col == route_row, 1.0, 0.0)
    place_col = jnp.sum(jnp.where(jj < ii, same, 0.0), axis=1, keepdims=True)
    place_row = jnp.sum(jnp.where(ii < jj, same, 0.0), axis=0, keepdims=True)
    slot_col = route_col * float(sent_rows) + place_col * 3.0
    slot_row = route_row[0:1, :] * float(reply_rows) + place_row
    own = (iota((count, taken), 1) >> 2) == iota((count, taken), 0)
    comp = iota((1, taken), 1) & 3
    at_row = jnp.sum(jnp.where(own, slot_col, 0.0), axis=0, keepdims=True)
    at_row = jnp.where(comp < 3, at_row + comp.astype(f32), -1.0)
    scatter_ref[...] = jnp.where(
        iota((spread, taken), 0).astype(f32) == at_row, 1.0, 0.0
    ).astype(bf16)
    own = (iota((taken, count), 0) >> 2) == iota((taken, count), 1)
    comp = iota((taken, 1), 0) & 3
    at_col = jnp.sum(jnp.where(own, slot_row, 0.0), axis=1, keepdims=True)
    at_col = jnp.where(comp < 3, at_col + 2.0 * comp.astype(f32), -1.0)
    slot_ref[...] = at_col
    to_peer = jnp.where(
        iota((peers, count), 0).astype(f32) == route_row[0:1, :], 1.0, 0.0
    )
    named = jnp.where(
        iota((count, meta_ref.shape[1]), 1).astype(f32) == place_col, target_col + 1.0, 0.0
    )
    tags = jnp.dot(to_peer.astype(bf16), named.astype(bf16), preferred_element_type=f32) - 1.0
    copies[2].wait()
    columns = diff_ref.shape[0]
    lanes = diff_ref.shape[3]
    sums = {}
    for m in range(columns):
        for n in range(m, columns):
            part = jnp.sum(diff_ref[m] * diff_ref[n], axis=0)
            sums[m, n] = jnp.sum(part, axis=0, keepdims=True)
    stacked = jnp.concatenate(
        [sums[min(m, n), max(m, n)] for m in range(columns) for n in range(columns)], axis=0
    )
    col = jnp.sum(stacked, axis=1, keepdims=True)
    diag = iota((columns * columns, lanes), 0) == iota((columns * columns, lanes), 1) - gram_lane
    gram = jnp.sum(jnp.where(diag, col, 0.0), axis=0, keepdims=True)
    meta_ref[...] = jnp.where(iota(meta_ref.shape, 1) < gram_lane, tags, gram)
    for copy in copies[3:] + later:
        copy.wait()
    bulk_ref[0] = dens_ref[0].astype(bf16)
    for c in range(3):
        bulk_ref[1 + c] = vel_ref[c, 0].astype(bf16)
    bulk_ref[4] = press_ref[0].astype(bf16)


def thirds(value):
    high = value.astype(bf16)
    rest = value - high.astype(f32)
    middle = rest.astype(bf16)
    return high, middle, (rest - middle.astype(f32)).astype(bf16)


def exact_dot(onehot, value):
    parts = jnp.concatenate(thirds(value), axis=1)
    made = jnp.dot(onehot, parts, preferred_element_type=f32)
    lanes = value.shape[1]
    return made[:, :lanes] + made[:, lanes : 2 * lanes] + made[:, 2 * lanes :]


def pick_half(both):
    lanes = both.shape[1] // 2
    return jnp.where(iota((8, lanes), 0) < 4, both[:, :lanes], both[:, lanes:])


def nt_dot(a, b):
    return lax.dot_general(a, b, (((1,), (1,)), ((), ())), preferred_element_type=f32)


def loads(
    start_ref, own_ref, below_ref, above_ref, corr_ref, normals_ref, rbf_ref,
    scatter_ref, meta_ref, send_ref, weighted, mapped,
):
    wall = wall_pressure(
        row_cell(start_ref), row_cell(own_ref), row_cell(below_ref), row_cell(above_ref)
    )
    count, nodes = corr_ref.shape
    at = corr_ref[...]
    within, part = at & (nodes - 1), at >> (nodes.bit_length() - 1)
    found = jnp.zeros((count, nodes), f32)
    for k in range(wall.shape[1] // nodes):
        table = jnp.broadcast_to(wall[:, k * nodes : (k + 1) * nodes], (count, nodes))
        got = jnp.take_along_axis(table, within, axis=1, mode="promise_in_bounds")
        found = jnp.where(part == k, got, found)
    for c in range(3):
        weighted[pl.ds(c, count, stride=4), :] = found * normals_ref[c]
    weighted[pl.ds(3, count, stride=4), :] = jnp.zeros((count, nodes), f32)
    for k in range(count // 2):
        both = jnp.concatenate([rbf_ref[2 * k], rbf_ref[2 * k + 1]], axis=1)
        left = weighted[8 * k : 8 * k + 8, :].astype(bf16)
        mapped[8 * k : 8 * k + 8, :] = pick_half(
            jnp.dot(left, both, preferred_element_type=f32)
        )
    send_ref[...] = exact_dot(scatter_ref[...], mapped[...])
    send_ref[pl.ds(sent_rows - 1, meta_ref.shape[0], stride=sent_rows), :] = meta_ref[...]


def solid(
    keep_ref, disp_ref, below_ref, stiff_hbm, coup_hbm, out_ref,
    stiff_ref, coup_ref, semaphores, here, prior, made,
):
    copies = fetch((stiff_hbm, coup_hbm), (stiff_ref, coup_ref), semaphores)
    count, nodes = disp_ref.shape[1:]
    for c in range(3):
        here[pl.ds(c, count, stride=4), :] = disp_ref[c]
        prior[pl.ds(4 + c, count, stride=4), :] = disp_ref[c]
        first = below_ref[5:6, c * nodes : (c + 1) * nodes]
        prior[c : c + 1, :] = jnp.where(keep_ref[0] > 0, first, 0.0)
    here[pl.ds(3, count, stride=4), :] = jnp.zeros((count, nodes), f32)
    prior[pl.ds(3, count + 1, stride=4), :] = jnp.zeros((count + 1, nodes), f32)
    for copy in copies:
        copy.wait()
    for k in range(count // 2):
        rows = slice(8 * k, 8 * k + 8)
        left = jnp.concatenate([here[rows, :], prior[rows, :]], axis=1).astype(bf16)
        right = jnp.concatenate(
            [
                jnp.concatenate([stiff_ref[2 * k], stiff_ref[2 * k + 1]], axis=0),
                jnp.concatenate([coup_ref[2 * k], coup_ref[2 * k + 1]], axis=0),
            ],
            axis=1,
        )
        made[rows, :] = pick_half(nt_dot(left, right))
    for c in range(3):
        out_ref[c] = made[pl.ds(c, count, stride=4), :]


def residual(got_ref, kd_ref, inv_ref, disp_ref, diff_ref, base_ref, share_ref):
    count, nodes = disp_ref.shape[1:]
    peers = share_ref.shape[0]
    turned = got_ref[pl.ds(sent_rows - 1, peers, stride=sent_rows), :].T
    block = iota((count, peers), 0).astype(f32)
    chosen = jnp.concatenate(
        [jnp.where(block == turned[i : i + 1, :], 1.0, 0.0) for i in range(2)], axis=1
    ).astype(bf16)
    res = []
    for c in range(3):
        rows = jnp.concatenate(
            [got_ref[pl.ds(c + 3 * i, peers, stride=sent_rows), :] for i in range(2)], axis=0
        )
        part = -inv_ref[c] * (kd_ref[c] - exact_dot(chosen, rows))
        base_ref[c] = disp_ref[c] + part
        res.append(part)
    columns = diff_ref.shape[0]
    sums = []
    for m in range(columns):
        part = sum(diff_ref[m, c] * res[c] for c in range(3))
        sums.append(jnp.sum(part, axis=0, keepdims=True))
    col = jnp.sum(jnp.concatenate(sums, axis=0), axis=1, keepdims=True)
    diag = iota((columns, nodes), 0) == iota((columns, nodes), 1)
    row = jnp.sum(jnp.where(diag, col, 0.0), axis=0, keepdims=True)
    share_ref[...] = jnp.broadcast_to(row, share_ref.shape)


def factor(
    blocks, got_ref, dd_hbm, inverse_ref, serve_ref, turned_ref, dd_ref, semaphores, spread
):
    copies = fetch((dd_hbm,), (dd_ref,), semaphores)
    lanes = serve_ref.shape[1]
    peers = serve_ref.shape[0] // reply_rows
    meta = got_ref[pl.ds(sent_rows - 1, peers, stride=sent_rows), :]
    block = iota((peers, lanes), 1).astype(f32)
    for i in range(2):
        tag = jnp.broadcast_to(meta[:, i : i + 1], (peers, lanes))
        for c in range(3):
            wanted = jnp.where(tag >= 0.0, tag + float(c * blocks), -1.0)
            hot = jnp.where(block == wanted, 1.0, 0.0)
            spread[pl.ds(2 * c + i, peers, stride=reply_rows), :] = hot
    serve_ref[...] = spread[...].astype(bf16)
    row = iota((8, lanes), 0)
    lane = iota((8, lanes), 1)
    total = jnp.sum(meta, axis=0, keepdims=True)
    total = pltpu.roll(total, lanes - gram_lane, 1)
    n = 8
    gram = jnp.concatenate(
        [total if m == 0 else pltpu.roll(total, lanes - n * m, 1) for m in range(n)], axis=0
    )
    work = jnp.where(lane < n, gram, jnp.where(lane == row + n, 1.0, 0.0))
    for k in range(n):
        pivot = work[k : k + 1, :] * lax.rsqrt(work[k : k + 1, k : k + 1])
        below = work[:, k : k + 1] * lax.rsqrt(work[k : k + 1, k : k + 1])
        work = jnp.where(row == k, pivot, jnp.where(row > k, work - below * pivot, work))
    inverse = jnp.where(lane < n, pltpu.roll(work, lanes - n, 1), 0.0)
    inverse_ref[...] = inverse
    copies[0].wait()
    for k in range(n):
        for c in range(3):
            turned_ref[k, c] = sum(
                inverse[k : k + 1, m : m + 1] * dd_ref[m, c] for m in range(k + 1)
            )


def update(share_ref, inverse_ref, base_ref, turned_ref, serve_ref, next_ref, reply_ref):
    projected = jnp.sum(share_ref[...], axis=0, keepdims=True)
    middle = jnp.sum(inverse_ref[...] * projected, axis=1, keepdims=True)
    rows = []
    for c in range(3):
        value = base_ref[c]
        for k in range(turned_ref.shape[0]):
            value = value - middle[k : k + 1, :] * turned_ref[k, c]
        next_ref[c] = value
        rows.append(value)
    blocks = jnp.concatenate(rows, axis=0).astype(bf16)
    spare = serve_ref.shape[1] - blocks.shape[0]
    blocks = jnp.concatenate([blocks, jnp.zeros((spare, blocks.shape[1]), bf16)], axis=0)
    reply_ref[...] = jnp.dot(
        serve_ref[...], blocks, preferred_element_type=f32
    ).astype(bf16)


def prepare(slot_ref, rbf_hbm, pick_ref, turned_ref, rbf_ref, semaphores):
    copies = fetch((rbf_hbm,), (rbf_ref,), semaphores)
    wanted = iota(pick_ref.shape, 1).astype(f32) == slot_ref[...]
    pick_ref[...] = jnp.where(wanted, 1.0, 0.0).astype(bf16)
    copies[0].wait()
    for b in range(rbf_ref.shape[0]):
        turned_ref[b] = rbf_ref[b].T


def motion(back_ref, pick_ref, turned_ref, out_ref, picked, made):
    count = turned_ref.shape[0]
    picked[...] = jnp.dot(pick_ref[...], back_ref[...], preferred_element_type=f32)
    for k in range(count // 2):
        rows = slice(8 * k, 8 * k + 8)
        both = jnp.concatenate([turned_ref[2 * k], turned_ref[2 * k + 1]], axis=1)
        left = picked[rows, :].astype(bf16)
        made[rows, :] = pick_half(jnp.dot(left, both, preferred_element_type=f32))
    for c in range(3):
        out_ref[c] = made[pl.ds(c, count, stride=4), :]


def exchange(value):
    return lax.all_to_all(value, AXES[::-1], split_axis=0, concat_axis=0, tiled=True)


def on_device(
    density, velocity, pressure, rbf, correlation, normals, routes, targets,
    stiffness, coupling, inverse_diag, displacement, diff_res, diff_disp,
):
    peers = lax.axis_size(AXES)
    depth, lanes = density.shape[1:]
    wide = -(-depth // 128) * 128
    count, nodes = correlation.shape
    blocks = displacement.shape[0]
    columns = diff_res.shape[0]
    normals, inverse_diag, displacement = (
        jnp.transpose(x, (1, 0, 2)) for x in (normals, inverse_diag, displacement)
    )
    diff_res, diff_disp = (jnp.transpose(x, (0, 2, 1, 3)) for x in (diff_res, diff_disp))
    ring = [(i, (i + 1) % peers) for i in range(peers)]
    back = [(j, i) for i, j in ring]

    own, second = call(
        edges,
        [shape((8, wide)), shape((8, wide))],
        density, velocity, pressure, displacement,
        fetched=(0, 1, 2, 3),
    )
    above = lax.ppermute(own, AXES, back)
    below = lax.ppermute(own, AXES, ring)
    kernel = functools.partial(routing, lax.axis_size(AXES[0]))
    kernel.__name__ = "routing"
    start, scatter, slot, meta, bulk, corr_near, normals_near, rbf_near = call(
        kernel,
        [
            shape((8, wide)),
            shape((sent_rows * peers, 4 * count), bf16),
            shape((4 * count, 1)),
            shape((peers, nodes)),
            shape((5, depth, lanes), bf16),
            shape(correlation.shape, jnp.int32),
            shape(normals.shape),
            shape(rbf.shape, bf16),
        ],
        routes.reshape(1, count), targets.reshape(1, count), diff_res,
        density, velocity, pressure, correlation, normals, rbf, own, second,
        fetched=(0, 1, 2, 3, 4, 5),
        remote=(6, 7, 8),
        scratch=[pltpu.SemaphoreType.DMA((3,))],
    )
    bulk_below = lax.ppermute(bulk, AXES, ring)
    bulk_above = lax.ppermute(bulk, AXES, back)
    sent = call(
        loads,
        shape((sent_rows * peers, nodes)),
        start, own, below, above, corr_near, normals_near, rbf_near, scatter, meta,
        scratch=[pltpu.VMEM((4 * count, nodes), f32)] * 2,
    )
    got = exchange(sent.reshape(peers, 1, sent_rows * nodes)).reshape(sent_rows * peers, nodes)
    keep = (lax.axis_index(AXES) > 0).astype(jnp.int32).reshape(1)
    product = call(
        solid,
        shape((3, blocks, nodes)),
        keep, displacement, below, stiffness, coupling,
        fetched=(3, 4),
        scalars=(0,),
        scratch=[
            pltpu.VMEM((4 * blocks, nodes), f32),
            pltpu.VMEM((4 * blocks + 8, nodes), f32),
            pltpu.VMEM((4 * blocks, nodes), f32),
        ],
    )
    base, share = call(
        residual,
        [shape((3, blocks, nodes)), shape((peers, nodes))],
        got, product, inverse_diag, displacement, diff_res,
    )
    shares = exchange(share)
    kernel = functools.partial(factor, blocks)
    kernel.__name__ = "factor"
    inverse, serve, turned = call(
        kernel,
        [
            shape((columns, nodes)),
            shape((reply_rows * peers, nodes), bf16),
            shape((columns, 3, blocks, nodes)),
        ],
        got, diff_disp,
        fetched=(1,),
        scratch=[pltpu.VMEM((reply_rows * peers, nodes), f32)],
    )
    disp_next, reply = call(
        update,
        [shape((3, blocks, nodes)), shape((reply_rows * peers, nodes), bf16)],
        shares, inverse, base, turned, serve,
    )
    reply = jnp.transpose(reply.reshape(peers, 3, 2, nodes), (0, 2, 1, 3))
    returned = exchange(reply.reshape(peers, 2, 3 * nodes)).reshape(peers, 2, 3, nodes)
    returned = jnp.transpose(returned, (0, 2, 1, 3)).reshape(reply_rows * peers, nodes)
    fluid_next = call(
        fluid,
        shape((5, 1, depth, lanes)),
        density, velocity, pressure, bulk_below, bulk_above,
        fetched=(0, 1, 2, 3, 4),
    )
    pick, rbf_turned = call(
        prepare,
        [shape((4 * count, reply_rows * peers), bf16), shape(rbf.shape, bf16)],
        slot, rbf,
        fetched=(1,),
    )
    wall_motion = call(
        motion,
        shape((3, count, nodes)),
        returned, pick, rbf_turned,
        scratch=[pltpu.VMEM((4 * count, nodes), f32)] * 2,
    )
    return (
        fluid_next,
        jnp.transpose(disp_next, (1, 0, 2)),
        jnp.transpose(wall_motion, (1, 0, 2)),
    )


def solution(mesh):
    rows = P(AXES, None, None)
    inner = P(None, AXES, None, None)
    return jax.shard_map(
        on_device,
        mesh=mesh,
        in_specs=(
            rows, inner, rows, rows, P(AXES, None), rows, P(AXES, None), P(AXES),
            rows, rows, rows, rows, inner, inner,
        ),
        out_specs=(inner, rows, rows),
        check_vma=False,
    )
```

```python
import functools

import jax
import jax.numpy as jnp
from jax import lax
from jax.experimental import pallas as pl
from jax.experimental.pallas import tpu as pltpu
from jax.sharding import PartitionSpec as P

AXES = ("group", "dev")
ratio_heat = 1.4
half_step = 0.5 * 0.03
f32 = jnp.float32
bf16 = jnp.bfloat16


def iota(shape, dim):
    return lax.broadcasted_iota(jnp.int32, shape, dim)


def call(kernel, out, *args, fetched=(), remote=(), scalars=(), scratch=(), out_specs=None, limit=48):
    held = (*fetched, *remote)
    buffers = [pltpu.VMEM(args[i].shape, args[i].dtype) for i in fetched]
    if fetched:
        buffers.append(pltpu.SemaphoreType.DMA((len(fetched),)))
    args = [
        pltpu.with_memory_space_constraint(x, pltpu.HBM) if i in held else x
        for i, x in enumerate(args)
    ]
    more = {} if out_specs is None else {"out_specs": out_specs}
    return pl.pallas_call(
        kernel,
        out_shape=out,
        **more,
        in_specs=[
            pl.BlockSpec(
                memory_space=pltpu.HBM
                if i in held
                else pltpu.SMEM
                if i in scalars
                else pltpu.VMEM
            )
            for i in range(len(args))
        ],
        scratch_shapes=buffers + list(scratch),
        compiler_params=pltpu.CompilerParams(vmem_limit_bytes=limit * 2**20),
        name=kernel.__name__,
    )(*args)


def fetch(sources, buffers, semaphores):
    copies = [
        pltpu.make_async_copy(source, buffer, semaphores.at[i])
        for i, (source, buffer) in enumerate(zip(sources, buffers))
    ]
    for copy in copies:
        copy.start()
    return copies


def shape(dims, dtype=f32):
    return jax.ShapeDtypeStruct(dims, dtype)


def conserve(cell):
    dens, v0, v1, v2, press = cell
    kinetic = v0 * v0 + v1 * v1 + v2 * v2
    energy = press * (1.0 / (ratio_heat - 1.0)) + 0.5 * dens * kinetic
    return (dens, dens * v0, dens * v1, dens * v2, energy)


def sound(cell):
    scaled = ratio_heat * cell[4]
    return scaled * lax.rsqrt(scaled * cell[0])


def with_speed(cell):
    return (cell, conserve(cell), sound(cell))


def euler_flux(state, axis):
    cell, cons, speed = state
    normal = cell[1 + axis]
    rows = [cons[1 + axis]]
    for comp in range(3):
        moment = cons[1 + comp] * normal
        rows.append(moment + cell[4] if comp == axis else moment)
    rows.append((cons[4] + cell[4]) * normal)
    return rows, jnp.abs(normal) + speed


def rusanov(left, right, axis):
    flux_left, speed_left = euler_flux(left, axis)
    flux_right, speed_right = euler_flux(right, axis)
    top = jnp.maximum(speed_left, speed_right)
    return [
        a + b - top * (r - l)
        for a, b, l, r in zip(flux_left, flux_right, left[1], right[1])
    ]


def divergence(left, me, right, axis):
    flux_left, speed_left = euler_flux(left, axis)
    flux_right, speed_right = euler_flux(right, axis)
    own = jnp.abs(me[0][1 + axis]) + me[2]
    low, high = jnp.maximum(speed_left, own), jnp.maximum(own, speed_right)
    return [
        b - a - high * (r - c) + low * (c - l)
        for a, b, l, c, r in zip(flux_left, flux_right, left[1], me[1], right[1])
    ]


def wall_flux(state):
    cell, cons, speed = state
    return 2.0 * (cons[3] * cell[3] + cell[4] - (jnp.abs(cell[3]) + speed) * cons[3])


def edges(
    dens_hbm, vel_hbm, press_hbm, disp_hbm, send_ref, second_ref,
    dens_ref, vel_ref, press_ref, disp_ref, semaphores,
):
    copies = fetch(
        (dens_hbm, vel_hbm, press_hbm, disp_hbm),
        (dens_ref, vel_ref, press_ref, disp_ref),
        semaphores,
    )
    depth, lanes = dens_ref.shape[1:]
    wide = send_ref.shape[1]
    lane = iota((depth, lanes), 1)
    packed = jnp.ones((depth, lanes), f32)
    rows = [
        (copies[0], dens_ref.at[0]),
        (copies[1], vel_ref.at[0, 0]),
        (None, vel_ref.at[1, 0]),
        (None, vel_ref.at[2, 0]),
        (copies[2], press_ref.at[0]),
    ]
    for i, (copy, ref) in enumerate(rows):
        if copy is not None:
            copy.wait()
        row = ref[...]
        moved = row if i == 0 else pltpu.roll(row, 2 * i, 1)
        packed = jnp.where((lane >> 1) == i, moved, packed)
    packed = jnp.concatenate([packed, jnp.ones((wide - depth, lanes), f32)], axis=0)
    turned = packed.T
    last = disp_ref.shape[1] - 1
    copies[3].wait()
    for i in range(5):
        send_ref[i : i + 1, :] = turned[2 * i : 2 * i + 1, :]
        second_ref[i : i + 1, :] = turned[2 * i + 1 : 2 * i + 2, :]
    nodes = disp_ref.shape[2]
    for c in range(3):
        send_ref[5:6, c * nodes : (c + 1) * nodes] = disp_ref[c, last : last + 1, :]
    send_ref[6:8, :] = jnp.zeros((2, wide), f32)
    second_ref[5:8, :] = jnp.zeros((3, wide), f32)


def fluid(
    dens_hbm, vel_hbm, press_hbm, below_hbm, above_hbm, next_ref,
    dens_ref, vel_ref, press_ref, below_ref, above_ref, semaphores,
):
    for copy in fetch(
        (dens_hbm, vel_hbm, press_hbm, below_hbm, above_hbm),
        (dens_ref, vel_ref, press_ref, below_ref, above_ref),
        semaphores,
    ):
        copy.wait()
    depth, lanes = dens_ref.shape[1:]
    rows = 16
    sub = iota((rows, lanes), 0)
    lane = iota((rows, lanes), 1)

    def load(at):
        return (
            dens_ref[0, at, :],
            vel_ref[0, 0, at, :],
            vel_ref[1, 0, at, :],
            vel_ref[2, 0, at, :],
            press_ref[0, at, :],
        )

    def step(i, carried):
        start = pl.multiple_of(i * rows, rows)
        after = pl.multiple_of(jnp.where(start + rows == depth, 0, start + rows), 8)
        at = pl.ds(start, rows)
        cell = load(at)
        ahead = load(pl.ds(after, 8))
        me = with_speed(cell)
        below = with_speed([below_ref[q, at, :].astype(f32) for q in range(5)])
        above = with_speed([above_ref[q, at, :].astype(f32) for q in range(5)])
        total = divergence(below, me, above, 0)
        beside = with_speed(
            [
                jnp.where(sub == rows - 1, n[0:1, :], pltpu.roll(x, rows - 1, 0))
                for x, n in zip(cell, ahead)
            ]
        )
        face = rusanov(me, beside, 1)
        total = [
            t + f - jnp.where(sub == 0, c, pltpu.roll(f, 1, 0))
            for t, f, c in zip(total, face, carried)
        ]
        carried = tuple(f[rows - 1 : rows, :] for f in face)
        over = with_speed(
            [jnp.where(lane == lanes - 1, x, pltpu.roll(x, lanes - 1, 1)) for x in cell]
        )
        face = rusanov(me, over, 2)
        wall = wall_flux(me)
        for q in range(5):
            lower = jnp.where(
                lane == 0, wall if q == 3 else 0.0, pltpu.roll(face[q], 1, 1)
            )
            next_ref[q, 0, at, :] = me[1][q] - half_step * (total[q] + face[q] - lower)
        return carried

    first = with_speed([x[0:1, :] for x in load(pl.ds(0, 8))])
    last = with_speed([x[7:8, :] for x in load(pl.ds(depth - 8, 8))])
    lax.fori_loop(0, depth // rows, step, tuple(rusanov(last, first, 1)))


def row_cell(ref):
    return [ref[i : i + 1, :] for i in range(5)]


def wall_start(depth, own, second):
    wide = own[0].shape[1]
    lane = iota((1, wide), 1)
    me = with_speed(own)

    def up(x):
        return jnp.where(lane == depth - 1, x[:, 0:1], pltpu.roll(x, wide - 1, 1))

    def down(x):
        return jnp.where(lane == 0, x[:, depth - 1 : depth], pltpu.roll(x, 1, 1))

    face = rusanov(me, with_speed([up(x) for x in own]), 1)
    total = [f - down(f) for f in face]
    face = rusanov(me, with_speed(second), 2)
    total = [t + f for t, f in zip(total, face)]
    total[3] = total[3] - wall_flux(me)
    return [c - half_step * t for c, t in zip(me[1], total)]


def wall_pressure(start, own, below, above):
    total = divergence(with_speed(below), with_speed(own), with_speed(above), 0)
    q = [c - half_step * t for c, t in zip(start, total)]
    return (ratio_heat - 1.0) * (
        q[4] - 0.5 * (q[1] * q[1] + q[2] * q[2] + q[3] * q[3]) / q[0]
    )


sent_rows = 7
reply_rows = 6
gram_lane = 64


def routing(
    groups, routes_hbm, targets_hbm, diff_hbm, dens_hbm, vel_hbm, press_hbm,
    corr_hbm, normals_hbm, rbf_hbm, own_ref, second_ref,
    start_ref, scatter_ref, slot_ref, meta_ref, bulk_ref, corr_ref, normals_ref, rbf_ref,
    routes_ref, targets_ref, diff_ref, dens_ref, vel_ref, press_ref, semaphores, ahead,
):
    copies = fetch(
        (routes_hbm, targets_hbm, diff_hbm, dens_hbm, vel_hbm, press_hbm),
        (routes_ref, targets_ref, diff_ref, dens_ref, vel_ref, press_ref),
        semaphores,
    )
    later = fetch((corr_hbm, normals_hbm, rbf_hbm), (corr_ref, normals_ref, rbf_ref), ahead)
    start = wall_start(dens_ref.shape[1], row_cell(own_ref), row_cell(second_ref))
    for i in range(5):
        start_ref[i : i + 1, :] = start[i]
    start_ref[5:8, :] = jnp.zeros((3, start_ref.shape[1]), f32)
    copies[0].wait()
    copies[1].wait()
    count = routes_ref.shape[1]
    spread, taken = scatter_ref.shape
    peers = meta_ref.shape[0]
    ii, jj = iota((count, count), 0), iota((count, count), 1)
    inner = peers // groups
    routes = routes_ref[...]
    routes = (routes & (inner - 1)) * groups + (routes >> (inner.bit_length() - 1))
    route_row = jnp.broadcast_to(routes, (count, count)).astype(f32)
    target_row = jnp.broadcast_to(targets_ref[...], (count, count)).astype(f32)
    route_col = jnp.sum(jnp.where(ii == jj, route_row, 0.0), axis=1, keepdims=True)
    target_col = jnp.sum(jnp.where(ii == jj, target_row, 0.0), axis=1, keepdims=True)
    same = jnp.where(route_col == route_row, 1.0, 0.0)
    place_col = jnp.sum(jnp.where(jj < ii, same, 0.0), axis=1, keepdims=True)
    place_row = jnp.sum(jnp.where(ii < jj, same, 0.0), axis=0, keepdims=True)
    slot_col = route_col * float(sent_rows) + place_col * 3.0
    slot_row = route_row[0:1, :] * float(reply_rows) + place_row
    own = (iota((count, taken), 1) >> 2) == iota((count, taken), 0)
    comp = iota((1, taken), 1) & 3
    at_row = jnp.sum(jnp.where(own, slot_col, 0.0), axis=0, keepdims=True)
    at_row = jnp.where(comp < 3, at_row + comp.astype(f32), -1.0)
    scatter_ref[...] = jnp.where(
        iota((spread, taken), 0).astype(f32) == at_row, 1.0, 0.0
    ).astype(bf16)
    own = (iota((taken, count), 0) >> 2) == iota((taken, count), 1)
    comp = iota((taken, 1), 0) & 3
    at_col = jnp.sum(jnp.where(own, slot_row, 0.0), axis=1, keepdims=True)
    at_col = jnp.where(comp < 3, at_col + 2.0 * comp.astype(f32), -1.0)
    slot_ref[...] = at_col
    to_peer = jnp.where(
        iota((peers, count), 0).astype(f32) == route_row[0:1, :], 1.0, 0.0
    )
    named = jnp.where(
        iota((count, meta_ref.shape[1]), 1).astype(f32) == place_col, target_col + 1.0, 0.0
    )
    tags = jnp.dot(to_peer.astype(bf16), named.astype(bf16), preferred_element_type=f32) - 1.0
    copies[2].wait()
    columns = diff_ref.shape[0]
    lanes = diff_ref.shape[3]
    sums = {}
    for m in range(columns):
        for n in range(m, columns):
            part = jnp.sum(diff_ref[m] * diff_ref[n], axis=0)
            sums[m, n] = jnp.sum(part, axis=0, keepdims=True)
    stacked = jnp.concatenate(
        [sums[min(m, n), max(m, n)] for m in range(columns) for n in range(columns)], axis=0
    )
    col = jnp.sum(stacked, axis=1, keepdims=True)
    diag = iota((columns * columns, lanes), 0) == iota((columns * columns, lanes), 1) - gram_lane
    gram = jnp.sum(jnp.where(diag, col, 0.0), axis=0, keepdims=True)
    meta_ref[...] = jnp.where(iota(meta_ref.shape, 1) < gram_lane, tags, gram)
    for copy in copies[3:] + later:
        copy.wait()
    bulk_ref[0] = dens_ref[0].astype(bf16)
    for c in range(3):
        bulk_ref[1 + c] = vel_ref[c, 0].astype(bf16)
    bulk_ref[4] = press_ref[0].astype(bf16)


def thirds(value):
    high = value.astype(bf16)
    rest = value - high.astype(f32)
    middle = rest.astype(bf16)
    return high, middle, (rest - middle.astype(f32)).astype(bf16)


def exact_dot(onehot, value):
    parts = jnp.concatenate(thirds(value), axis=1)
    made = jnp.dot(onehot, parts, preferred_element_type=f32)
    lanes = value.shape[1]
    return made[:, :lanes] + made[:, lanes : 2 * lanes] + made[:, 2 * lanes :]


def pick_half(both):
    lanes = both.shape[1] // 2
    return jnp.where(iota((8, lanes), 0) < 4, both[:, :lanes], both[:, lanes:])


def nt_dot(a, b):
    return lax.dot_general(a, b, (((1,), (1,)), ((), ())), preferred_element_type=f32)


def loads(
    start_ref, own_ref, below_ref, above_ref, corr_ref, normals_ref, rbf_ref,
    scatter_ref, meta_ref, send_hbm, weighted, mapped, made_ref, semaphores,
):
    wall = wall_pressure(
        row_cell(start_ref), row_cell(own_ref), row_cell(below_ref), row_cell(above_ref)
    )
    count, nodes = corr_ref.shape
    at = corr_ref[...]
    within, part = at & (nodes - 1), at >> (nodes.bit_length() - 1)
    found = jnp.zeros((count, nodes), f32)
    for k in range(wall.shape[1] // nodes):
        table = jnp.broadcast_to(wall[:, k * nodes : (k + 1) * nodes], (count, nodes))
        got = jnp.take_along_axis(table, within, axis=1, mode="promise_in_bounds")
        found = jnp.where(part == k, got, found)
    for c in range(3):
        weighted[pl.ds(c, count, stride=4), :] = found * normals_ref[c]
    weighted[pl.ds(3, count, stride=4), :] = jnp.zeros((count, nodes), f32)
    for k in range(count // 2):
        both = jnp.concatenate([rbf_ref[2 * k], rbf_ref[2 * k + 1]], axis=1)
        left = weighted[8 * k : 8 * k + 8, :].astype(bf16)
        mapped[8 * k : 8 * k + 8, :] = pick_half(
            jnp.dot(left, both, preferred_element_type=f32)
        )
    peers = meta_ref.shape[0]
    parts = jnp.concatenate(thirds(mapped[...]), axis=1)
    share = peers // 4
    copies = []
    for i in range(4):
        rows = slice(i * share * sent_rows, (i + 1) * share * sent_rows)
        made = jnp.dot(scatter_ref[rows, :], parts, preferred_element_type=f32)
        made_ref[rows, :] = made[:, :nodes] + made[:, nodes : 2 * nodes] + made[:, 2 * nodes :]
        at = pl.ds((i * share + 1) * sent_rows - 1, share, stride=sent_rows)
        made_ref[at, :] = meta_ref[i * share : (i + 1) * share, :]
        copies.append(
            pltpu.make_async_copy(made_ref.at[rows, :], send_hbm.at[rows, :], semaphores.at[i])
        )
        copies[-1].start()
    for copy in copies:
        copy.wait()


def solid(
    keep_ref, disp_ref, below_ref, stiff_hbm, coup_hbm, out_ref,
    stiff_ref, coup_ref, semaphores, here, prior, made,
):
    copies = fetch((stiff_hbm, coup_hbm), (stiff_ref, coup_ref), semaphores)
    count, nodes = disp_ref.shape[1:]
    for c in range(3):
        here[pl.ds(c, count, stride=4), :] = disp_ref[c]
        prior[pl.ds(4 + c, count, stride=4), :] = disp_ref[c]
        first = below_ref[5:6, c * nodes : (c + 1) * nodes]
        prior[c : c + 1, :] = jnp.where(keep_ref[0] > 0, first, 0.0)
    here[pl.ds(3, count, stride=4), :] = jnp.zeros((count, nodes), f32)
    prior[pl.ds(3, count + 1, stride=4), :] = jnp.zeros((count + 1, nodes), f32)
    for copy in copies:
        copy.wait()
    for k in range(count // 2):
        rows = slice(8 * k, 8 * k + 8)
        left = jnp.concatenate([here[rows, :], prior[rows, :]], axis=1).astype(bf16)
        right = jnp.concatenate(
            [
                jnp.concatenate([stiff_ref[2 * k], stiff_ref[2 * k + 1]], axis=0),
                jnp.concatenate([coup_ref[2 * k], coup_ref[2 * k + 1]], axis=0),
            ],
            axis=1,
        )
        made[rows, :] = pick_half(nt_dot(left, right))
    for c in range(3):
        out_ref[c] = made[pl.ds(c, count, stride=4), :]


def residual(got_ref, kd_ref, inv_ref, disp_ref, diff_ref, base_ref, share_ref):
    count, nodes = disp_ref.shape[1:]
    peers = share_ref.shape[0]
    turned = got_ref[pl.ds(sent_rows - 1, peers, stride=sent_rows), :].T
    block = iota((count, peers), 0).astype(f32)
    chosen = jnp.concatenate(
        [jnp.where(block == turned[i : i + 1, :], 1.0, 0.0) for i in range(2)], axis=1
    ).astype(bf16)
    res = []
    for c in range(3):
        rows = jnp.concatenate(
            [got_ref[pl.ds(c + 3 * i, peers, stride=sent_rows), :] for i in range(2)], axis=0
        )
        part = -inv_ref[c] * (kd_ref[c] - exact_dot(chosen, rows))
        base_ref[c] = disp_ref[c] + part
        res.append(part)
    columns = diff_ref.shape[0]
    sums = []
    for m in range(columns):
        part = sum(diff_ref[m, c] * res[c] for c in range(3))
        sums.append(jnp.sum(part, axis=0, keepdims=True))
    col = jnp.sum(jnp.concatenate(sums, axis=0), axis=1, keepdims=True)
    diag = iota((columns, nodes), 0) == iota((columns, nodes), 1)
    row = jnp.sum(jnp.where(diag, col, 0.0), axis=0, keepdims=True)
    share_ref[...] = jnp.broadcast_to(row, share_ref.shape)


def factor(
    blocks, got_ref, dd_hbm, inverse_ref, serve_ref, turned_ref, dd_ref, semaphores, spread
):
    copies = fetch((dd_hbm,), (dd_ref,), semaphores)
    lanes = serve_ref.shape[1]
    peers = serve_ref.shape[0] // reply_rows
    meta = got_ref[pl.ds(sent_rows - 1, peers, stride=sent_rows), :]
    block = iota((peers, lanes), 1).astype(f32)
    for i in range(2):
        tag = jnp.broadcast_to(meta[:, i : i + 1], (peers, lanes))
        for c in range(3):
            wanted = jnp.where(tag >= 0.0, tag + float(c * blocks), -1.0)
            hot = jnp.where(block == wanted, 1.0, 0.0)
            spread[pl.ds(2 * c + i, peers, stride=reply_rows), :] = hot
    serve_ref[...] = spread[...].astype(bf16)
    row = iota((8, lanes), 0)
    lane = iota((8, lanes), 1)
    total = jnp.sum(meta, axis=0, keepdims=True)
    total = pltpu.roll(total, lanes - gram_lane, 1)
    n = 8
    gram = jnp.concatenate(
        [total if m == 0 else pltpu.roll(total, lanes - n * m, 1) for m in range(n)], axis=0
    )
    work = jnp.where(lane < n, gram, jnp.where(lane == row + n, 1.0, 0.0))
    for k in range(n):
        pivot = work[k : k + 1, :] * lax.rsqrt(work[k : k + 1, k : k + 1])
        below = work[:, k : k + 1] * lax.rsqrt(work[k : k + 1, k : k + 1])
        work = jnp.where(row == k, pivot, jnp.where(row > k, work - below * pivot, work))
    inverse = jnp.where(lane < n, pltpu.roll(work, lanes - n, 1), 0.0)
    inverse_ref[...] = inverse
    copies[0].wait()
    for k in range(n):
        for c in range(3):
            turned_ref[k, c] = sum(
                inverse[k : k + 1, m : m + 1] * dd_ref[m, c] for m in range(k + 1)
            )


def update(share_ref, inverse_ref, base_ref, turned_ref, serve_ref, next_ref, reply_ref):
    projected = jnp.sum(share_ref[...], axis=0, keepdims=True)
    middle = jnp.sum(inverse_ref[...] * projected, axis=1, keepdims=True)
    rows = []
    for c in range(3):
        value = base_ref[c]
        for k in range(turned_ref.shape[0]):
            value = value - middle[k : k + 1, :] * turned_ref[k, c]
        next_ref[c] = value
        rows.append(value)
    blocks = jnp.concatenate(rows, axis=0).astype(bf16)
    spare = serve_ref.shape[1] - blocks.shape[0]
    blocks = jnp.concatenate([blocks, jnp.zeros((spare, blocks.shape[1]), bf16)], axis=0)
    reply_ref[...] = jnp.dot(
        serve_ref[...], blocks, preferred_element_type=f32
    ).astype(bf16)


def prepare(slot_ref, rbf_hbm, pick_ref, turned_ref, rbf_ref, semaphores):
    copies = fetch((rbf_hbm,), (rbf_ref,), semaphores)
    wanted = iota(pick_ref.shape, 1).astype(f32) == slot_ref[...]
    pick_ref[...] = jnp.where(wanted, 1.0, 0.0).astype(bf16)
    copies[0].wait()
    for b in range(rbf_ref.shape[0]):
        turned_ref[b] = rbf_ref[b].T


def motion(back_ref, pick_ref, turned_ref, out_ref, picked, made):
    count = turned_ref.shape[0]
    picked[...] = jnp.dot(pick_ref[...], back_ref[...], preferred_element_type=f32)
    for k in range(count // 2):
        rows = slice(8 * k, 8 * k + 8)
        both = jnp.concatenate([turned_ref[2 * k], turned_ref[2 * k + 1]], axis=1)
        left = picked[rows, :].astype(bf16)
        made[rows, :] = pick_half(jnp.dot(left, both, preferred_element_type=f32))
    for c in range(3):
        out_ref[c] = made[pl.ds(c, count, stride=4), :]


def exchange(value):
    return lax.all_to_all(value, AXES[::-1], split_axis=0, concat_axis=0, tiled=True)


def on_device(
    density, velocity, pressure, rbf, correlation, normals, routes, targets,
    stiffness, coupling, inverse_diag, displacement, diff_res, diff_disp,
):
    peers = lax.axis_size(AXES)
    depth, lanes = density.shape[1:]
    wide = -(-depth // 128) * 128
    count, nodes = correlation.shape
    blocks = displacement.shape[0]
    columns = diff_res.shape[0]
    normals, inverse_diag, displacement = (
        jnp.transpose(x, (1, 0, 2)) for x in (normals, inverse_diag, displacement)
    )
    diff_res, diff_disp = (jnp.transpose(x, (0, 2, 1, 3)) for x in (diff_res, diff_disp))
    ring = [(i, (i + 1) % peers) for i in range(peers)]
    back = [(j, i) for i, j in ring]

    own, second = call(
        edges,
        [shape((8, wide)), shape((8, wide))],
        density, velocity, pressure, displacement,
        fetched=(0, 1, 2, 3),
    )
    above = lax.ppermute(own, AXES, back)
    below = lax.ppermute(own, AXES, ring)
    kernel = functools.partial(routing, lax.axis_size(AXES[0]))
    kernel.__name__ = "routing"
    start, scatter, slot, meta, bulk, corr_near, normals_near, rbf_near = call(
        kernel,
        [
            shape((8, wide)),
            shape((sent_rows * peers, 4 * count), bf16),
            shape((4 * count, 1)),
            shape((peers, nodes)),
            shape((5, depth, lanes), bf16),
            shape(correlation.shape, jnp.int32),
            shape(normals.shape),
            shape(rbf.shape, bf16),
        ],
        routes.reshape(1, count), targets.reshape(1, count), diff_res,
        density, velocity, pressure, correlation, normals, rbf, own, second,
        fetched=(0, 1, 2, 3, 4, 5),
        remote=(6, 7, 8),
        scratch=[pltpu.SemaphoreType.DMA((3,))],
    )
    bulk_below = lax.ppermute(bulk, AXES, ring)
    bulk_above = lax.ppermute(bulk, AXES, back)
    sent = call(
        loads,
        shape((sent_rows * peers, nodes)),
        start, own, below, above, corr_near, normals_near, rbf_near, scatter, meta,
        scratch=[
            pltpu.VMEM((4 * count, nodes), f32),
            pltpu.VMEM((4 * count, nodes), f32),
            pltpu.VMEM((sent_rows * peers, nodes), f32),
            pltpu.SemaphoreType.DMA((4,)),
        ],
        out_specs=pl.BlockSpec(memory_space=pltpu.HBM),
    )
    got = exchange(sent.reshape(peers, 1, sent_rows * nodes)).reshape(sent_rows * peers, nodes)
    keep = (lax.axis_index(AXES) > 0).astype(jnp.int32).reshape(1)
    product = call(
        solid,
        shape((3, blocks, nodes)),
        keep, displacement, below, stiffness, coupling,
        fetched=(3, 4),
        scalars=(0,),
        scratch=[
            pltpu.VMEM((4 * blocks, nodes), f32),
            pltpu.VMEM((4 * blocks + 8, nodes), f32),
            pltpu.VMEM((4 * blocks, nodes), f32),
        ],
    )
    base, share = call(
        residual,
        [shape((3, blocks, nodes)), shape((peers, nodes))],
        got, product, inverse_diag, displacement, diff_res,
    )
    shares = exchange(share)
    kernel = functools.partial(factor, blocks)
    kernel.__name__ = "factor"
    inverse, serve, turned = call(
        kernel,
        [
            shape((columns, nodes)),
            shape((reply_rows * peers, nodes), bf16),
            shape((columns, 3, blocks, nodes)),
        ],
        got, diff_disp,
        fetched=(1,),
        scratch=[pltpu.VMEM((reply_rows * peers, nodes), f32)],
    )
    disp_next, reply = call(
        update,
        [shape((3, blocks, nodes)), shape((reply_rows * peers, nodes), bf16)],
        shares, inverse, base, turned, serve,
    )
    reply = jnp.transpose(reply.reshape(peers, 3, 2, nodes), (0, 2, 1, 3))
    returned = exchange(reply.reshape(peers, 2, 3 * nodes)).reshape(peers, 2, 3, nodes)
    returned = jnp.transpose(returned, (0, 2, 1, 3)).reshape(reply_rows * peers, nodes)
    fluid_next = call(
        fluid,
        shape((5, 1, depth, lanes)),
        density, velocity, pressure, bulk_below, bulk_above,
        fetched=(0, 1, 2, 3, 4),
    )
    pick, rbf_turned = call(
        prepare,
        [shape((4 * count, reply_rows * peers), bf16), shape(rbf.shape, bf16)],
        slot, rbf,
        fetched=(1,),
    )
    wall_motion = call(
        motion,
        shape((3, count, nodes)),
        returned, pick, rbf_turned,
        scratch=[pltpu.VMEM((4 * count, nodes), f32)] * 2,
    )
    return (
        fluid_next,
        jnp.transpose(disp_next, (1, 0, 2)),
        jnp.transpose(wall_motion, (1, 0, 2)),
    )


def solution(mesh):
    rows = P(AXES, None, None)
    inner = P(None, AXES, None, None)
    return jax.shard_map(
        on_device,
        mesh=mesh,
        in_specs=(
            rows, inner, rows, rows, P(AXES, None), rows, P(AXES, None), P(AXES),
            rows, rows, rows, rows, inner, inner,
        ),
        out_specs=(inner, rows, rows),
        check_vma=False,
    )
```

```python
import functools

import jax
import jax.numpy as jnp
from jax import lax
from jax.experimental import pallas as pl
from jax.experimental.pallas import tpu as pltpu
from jax.sharding import PartitionSpec as P

AXES = ("group", "dev")
ratio_heat = 1.4
half_step = 0.5 * 0.03
f32 = jnp.float32
bf16 = jnp.bfloat16


def iota(shape, dim):
    return lax.broadcasted_iota(jnp.int32, shape, dim)


def call(kernel, out, *args, fetched=(), remote=(), scalars=(), scratch=(), limit=48):
    held = (*fetched, *remote)
    buffers = [pltpu.VMEM(args[i].shape, args[i].dtype) for i in fetched]
    if fetched:
        buffers.append(pltpu.SemaphoreType.DMA((len(fetched),)))
    args = [
        pltpu.with_memory_space_constraint(x, pltpu.HBM) if i in held else x
        for i, x in enumerate(args)
    ]
    return pl.pallas_call(
        kernel,
        out_shape=out,
        in_specs=[
            pl.BlockSpec(
                memory_space=pltpu.HBM
                if i in held
                else pltpu.SMEM
                if i in scalars
                else pltpu.VMEM
            )
            for i in range(len(args))
        ],
        scratch_shapes=buffers + list(scratch),
        compiler_params=pltpu.CompilerParams(vmem_limit_bytes=limit * 2**20),
        name=kernel.__name__,
    )(*args)


def fetch(sources, buffers, semaphores):
    copies = [
        pltpu.make_async_copy(source, buffer, semaphores.at[i])
        for i, (source, buffer) in enumerate(zip(sources, buffers))
    ]
    for copy in copies:
        copy.start()
    return copies


def shape(dims, dtype=f32):
    return jax.ShapeDtypeStruct(dims, dtype)


def conserve(cell):
    dens, v0, v1, v2, press = cell
    kinetic = v0 * v0 + v1 * v1 + v2 * v2
    energy = press * (1.0 / (ratio_heat - 1.0)) + 0.5 * dens * kinetic
    return (dens, dens * v0, dens * v1, dens * v2, energy)


def sound(cell):
    scaled = ratio_heat * cell[4]
    return scaled * lax.rsqrt(scaled * cell[0])


def with_speed(cell):
    return (cell, conserve(cell), sound(cell))


def euler_flux(state, axis):
    cell, cons, speed = state
    normal = cell[1 + axis]
    rows = [cons[1 + axis]]
    for comp in range(3):
        moment = cons[1 + comp] * normal
        rows.append(moment + cell[4] if comp == axis else moment)
    rows.append((cons[4] + cell[4]) * normal)
    return rows, jnp.abs(normal) + speed


def rusanov(left, right, axis):
    flux_left, speed_left = euler_flux(left, axis)
    flux_right, speed_right = euler_flux(right, axis)
    top = jnp.maximum(speed_left, speed_right)
    return [
        a + b - top * (r - l)
        for a, b, l, r in zip(flux_left, flux_right, left[1], right[1])
    ]


def divergence(left, me, right, axis):
    flux_left, speed_left = euler_flux(left, axis)
    flux_right, speed_right = euler_flux(right, axis)
    own = jnp.abs(me[0][1 + axis]) + me[2]
    low, high = jnp.maximum(speed_left, own), jnp.maximum(own, speed_right)
    return [
        b - a - high * (r - c) + low * (c - l)
        for a, b, l, c, r in zip(flux_left, flux_right, left[1], me[1], right[1])
    ]


def wall_flux(state):
    cell, cons, speed = state
    return 2.0 * (cons[3] * cell[3] + cell[4] - (jnp.abs(cell[3]) + speed) * cons[3])


def edges(
    dens_hbm, vel_hbm, press_hbm, disp_hbm, send_ref, second_ref,
    dens_ref, vel_ref, press_ref, disp_ref, semaphores,
):
    copies = fetch(
        (dens_hbm, vel_hbm, press_hbm, disp_hbm),
        (dens_ref, vel_ref, press_ref, disp_ref),
        semaphores,
    )
    depth, lanes = dens_ref.shape[1:]
    wide = send_ref.shape[1]
    lane = iota((depth, lanes), 1)
    packed = jnp.ones((depth, lanes), f32)
    rows = [
        (copies[0], dens_ref.at[0]),
        (copies[1], vel_ref.at[0, 0]),
        (None, vel_ref.at[1, 0]),
        (None, vel_ref.at[2, 0]),
        (copies[2], press_ref.at[0]),
    ]
    for i, (copy, ref) in enumerate(rows):
        if copy is not None:
            copy.wait()
        row = ref[...]
        moved = row if i == 0 else pltpu.roll(row, 2 * i, 1)
        packed = jnp.where((lane >> 1) == i, moved, packed)
    packed = jnp.concatenate([packed, jnp.ones((wide - depth, lanes), f32)], axis=0)
    turned = packed.T
    last = disp_ref.shape[1] - 1
    copies[3].wait()
    for i in range(5):
        send_ref[i : i + 1, :] = turned[2 * i : 2 * i + 1, :]
        second_ref[i : i + 1, :] = turned[2 * i + 1 : 2 * i + 2, :]
    nodes = disp_ref.shape[2]
    for c in range(3):
        send_ref[5:6, c * nodes : (c + 1) * nodes] = disp_ref[c, last : last + 1, :]
    send_ref[6:8, :] = jnp.zeros((2, wide), f32)
    second_ref[5:8, :] = jnp.zeros((3, wide), f32)


def fluid(
    dens_hbm, vel_hbm, press_hbm, below_hbm, above_hbm, next_ref,
    dens_ref, vel_ref, press_ref, below_ref, above_ref, semaphores,
):
    for copy in fetch(
        (dens_hbm, vel_hbm, press_hbm, below_hbm, above_hbm),
        (dens_ref, vel_ref, press_ref, below_ref, above_ref),
        semaphores,
    ):
        copy.wait()
    depth, lanes = dens_ref.shape[1:]
    rows = 16
    sub = iota((rows, lanes), 0)
    lane = iota((rows, lanes), 1)

    def load(at):
        return (
            dens_ref[0, at, :],
            vel_ref[0, 0, at, :],
            vel_ref[1, 0, at, :],
            vel_ref[2, 0, at, :],
            press_ref[0, at, :],
        )

    def step(i, carried):
        start = pl.multiple_of(i * rows, rows)
        after = pl.multiple_of(jnp.where(start + rows == depth, 0, start + rows), 8)
        at = pl.ds(start, rows)
        cell = load(at)
        ahead = load(pl.ds(after, 8))
        me = with_speed(cell)
        below = with_speed([below_ref[q, at, :].astype(f32) for q in range(5)])
        above = with_speed([above_ref[q, at, :].astype(f32) for q in range(5)])
        total = divergence(below, me, above, 0)
        beside = with_speed(
            [
                jnp.where(sub == rows - 1, n[0:1, :], pltpu.roll(x, rows - 1, 0))
                for x, n in zip(cell, ahead)
            ]
        )
        face = rusanov(me, beside, 1)
        total = [
            t + f - jnp.where(sub == 0, c, pltpu.roll(f, 1, 0))
            for t, f, c in zip(total, face, carried)
        ]
        carried = tuple(f[rows - 1 : rows, :] for f in face)
        over = with_speed(
            [jnp.where(lane == lanes - 1, x, pltpu.roll(x, lanes - 1, 1)) for x in cell]
        )
        face = rusanov(me, over, 2)
        wall = wall_flux(me)
        for q in range(5):
            lower = jnp.where(
                lane == 0, wall if q == 3 else 0.0, pltpu.roll(face[q], 1, 1)
            )
            next_ref[q, 0, at, :] = me[1][q] - half_step * (total[q] + face[q] - lower)
        return carried

    first = with_speed([x[0:1, :] for x in load(pl.ds(0, 8))])
    last = with_speed([x[7:8, :] for x in load(pl.ds(depth - 8, 8))])
    lax.fori_loop(0, depth // rows, step, tuple(rusanov(last, first, 1)))


def row_cell(ref):
    return [ref[i : i + 1, :] for i in range(5)]


def wall_start(depth, own, second):
    wide = own[0].shape[1]
    lane = iota((1, wide), 1)
    me = with_speed(own)

    def up(x):
        return jnp.where(lane == depth - 1, x[:, 0:1], pltpu.roll(x, wide - 1, 1))

    def down(x):
        return jnp.where(lane == 0, x[:, depth - 1 : depth], pltpu.roll(x, 1, 1))

    face = rusanov(me, with_speed([up(x) for x in own]), 1)
    total = [f - down(f) for f in face]
    face = rusanov(me, with_speed(second), 2)
    total = [t + f for t, f in zip(total, face)]
    total[3] = total[3] - wall_flux(me)
    return [c - half_step * t for c, t in zip(me[1], total)]


def wall_pressure(start, own, below, above):
    total = divergence(with_speed(below), with_speed(own), with_speed(above), 0)
    q = [c - half_step * t for c, t in zip(start, total)]
    return (ratio_heat - 1.0) * (
        q[4] - 0.5 * (q[1] * q[1] + q[2] * q[2] + q[3] * q[3]) / q[0]
    )


sent_rows = 7
reply_rows = 6
gram_lane = 64


def routing(
    groups, routes_hbm, targets_hbm, diff_hbm, dens_hbm, vel_hbm, press_hbm,
    corr_hbm, normals_hbm, rbf_hbm, own_ref, second_ref,
    start_ref, scatter_ref, slot_ref, meta_ref, bulk_ref, corr_ref, normals_ref, rbf_ref,
    routes_ref, targets_ref, diff_ref, dens_ref, vel_ref, press_ref, semaphores, ahead,
):
    copies = fetch(
        (routes_hbm, targets_hbm, diff_hbm, dens_hbm, vel_hbm, press_hbm),
        (routes_ref, targets_ref, diff_ref, dens_ref, vel_ref, press_ref),
        semaphores,
    )
    later = fetch((corr_hbm, normals_hbm, rbf_hbm), (corr_ref, normals_ref, rbf_ref), ahead)
    start = wall_start(dens_ref.shape[1], row_cell(own_ref), row_cell(second_ref))
    for i in range(5):
        start_ref[i : i + 1, :] = start[i]
    start_ref[5:8, :] = jnp.zeros((3, start_ref.shape[1]), f32)
    copies[0].wait()
    copies[1].wait()
    count = routes_ref.shape[1]
    spread, taken = scatter_ref.shape
    peers = meta_ref.shape[0]
    ii, jj = iota((count, count), 0), iota((count, count), 1)
    inner = peers // groups
    routes = routes_ref[...]
    routes = (routes & (inner - 1)) * groups + (routes >> (inner.bit_length() - 1))
    route_row = jnp.broadcast_to(routes, (count, count)).astype(f32)
    target_row = jnp.broadcast_to(targets_ref[...], (count, count)).astype(f32)
    route_col = jnp.sum(jnp.where(ii == jj, route_row, 0.0), axis=1, keepdims=True)
    target_col = jnp.sum(jnp.where(ii == jj, target_row, 0.0), axis=1, keepdims=True)
    same = jnp.where(route_col == route_row, 1.0, 0.0)
    place_col = jnp.sum(jnp.where(jj < ii, same, 0.0), axis=1, keepdims=True)
    place_row = jnp.sum(jnp.where(ii < jj, same, 0.0), axis=0, keepdims=True)
    slot_col = route_col * float(sent_rows) + place_col * 3.0
    slot_row = route_row[0:1, :] * float(reply_rows) + place_row
    own = (iota((count, taken), 1) >> 2) == iota((count, taken), 0)
    comp = iota((1, taken), 1) & 3
    at_row = jnp.sum(jnp.where(own, slot_col, 0.0), axis=0, keepdims=True)
    at_row = jnp.where(comp < 3, at_row + comp.astype(f32), -1.0)
    scatter_ref[...] = jnp.where(
        iota((spread, taken), 0).astype(f32) == at_row, 1.0, 0.0
    ).astype(bf16)
    own = (iota((taken, count), 0) >> 2) == iota((taken, count), 1)
    comp = iota((taken, 1), 0) & 3
    at_col = jnp.sum(jnp.where(own, slot_row, 0.0), axis=1, keepdims=True)
    at_col = jnp.where(comp < 3, at_col + 2.0 * comp.astype(f32), -1.0)
    slot_ref[...] = at_col
    to_peer = jnp.where(
        iota((peers, count), 0).astype(f32) == route_row[0:1, :], 1.0, 0.0
    )
    named = jnp.where(
        iota((count, meta_ref.shape[1]), 1).astype(f32) == place_col, target_col + 1.0, 0.0
    )
    tags = jnp.dot(to_peer.astype(bf16), named.astype(bf16), preferred_element_type=f32) - 1.0
    copies[2].wait()
    columns = diff_ref.shape[0]
    lanes = diff_ref.shape[3]
    sums = {}
    for m in range(columns):
        for n in range(m, columns):
            part = jnp.sum(diff_ref[m] * diff_ref[n], axis=0)
            sums[m, n] = jnp.sum(part, axis=0, keepdims=True)
    stacked = jnp.concatenate(
        [sums[min(m, n), max(m, n)] for m in range(columns) for n in range(columns)], axis=0
    )
    col = jnp.sum(stacked, axis=1, keepdims=True)
    diag = iota((columns * columns, lanes), 0) == iota((columns * columns, lanes), 1) - gram_lane
    gram = jnp.sum(jnp.where(diag, col, 0.0), axis=0, keepdims=True)
    meta_ref[...] = jnp.where(iota(meta_ref.shape, 1) < gram_lane, tags, gram)
    for copy in copies[3:] + later:
        copy.wait()
    bulk_ref[0] = dens_ref[0].astype(bf16)
    for c in range(3):
        bulk_ref[1 + c] = vel_ref[c, 0].astype(bf16)
    bulk_ref[4] = press_ref[0].astype(bf16)


def thirds(value):
    high = value.astype(bf16)
    rest = value - high.astype(f32)
    middle = rest.astype(bf16)
    return high, middle, (rest - middle.astype(f32)).astype(bf16)


def exact_dot(onehot, value):
    parts = jnp.concatenate(thirds(value), axis=1)
    made = jnp.dot(onehot, parts, preferred_element_type=f32)
    lanes = value.shape[1]
    return made[:, :lanes] + made[:, lanes : 2 * lanes] + made[:, 2 * lanes :]


def pick_half(both):
    lanes = both.shape[1] // 2
    return jnp.where(iota((8, lanes), 0) < 4, both[:, :lanes], both[:, lanes:])


def nt_dot(a, b):
    return lax.dot_general(a, b, (((1,), (1,)), ((), ())), preferred_element_type=f32)


def loads(
    start_ref, own_ref, below_ref, above_ref, corr_ref, normals_ref, rbf_ref,
    scatter_ref, meta_ref, product_ref, send_ref, weighted, mapped,
):
    wall = wall_pressure(
        row_cell(start_ref), row_cell(own_ref), row_cell(below_ref), row_cell(above_ref)
    )
    count, nodes = corr_ref.shape
    at = corr_ref[...]
    within, part = at & (nodes - 1), at >> (nodes.bit_length() - 1)
    found = jnp.zeros((count, nodes), f32)
    for k in range(wall.shape[1] // nodes):
        table = jnp.broadcast_to(wall[:, k * nodes : (k + 1) * nodes], (count, nodes))
        got = jnp.take_along_axis(table, within, axis=1, mode="promise_in_bounds")
        found = jnp.where(part == k, got, found)
    for c in range(3):
        weighted[pl.ds(c, count, stride=4), :] = found * normals_ref[c]
    weighted[pl.ds(3, count, stride=4), :] = jnp.zeros((count, nodes), f32)
    for k in range(count // 2):
        both = jnp.concatenate([rbf_ref[2 * k], rbf_ref[2 * k + 1]], axis=1)
        left = weighted[8 * k : 8 * k + 8, :].astype(bf16)
        mapped[8 * k : 8 * k + 8, :] = pick_half(
            jnp.dot(left, both, preferred_element_type=f32)
        )
    send_ref[...] = exact_dot(scatter_ref[...], mapped[...])
    send_ref[pl.ds(sent_rows - 1, meta_ref.shape[0], stride=sent_rows), :] = meta_ref[...]


def solid(
    keep_ref, disp_ref, below_ref, stiff_hbm, coup_hbm, out_ref,
    stiff_ref, coup_ref, semaphores, here, prior, made,
):
    copies = fetch((stiff_hbm, coup_hbm), (stiff_ref, coup_ref), semaphores)
    count, nodes = disp_ref.shape[1:]
    for c in range(3):
        here[pl.ds(c, count, stride=4), :] = disp_ref[c]
        prior[pl.ds(4 + c, count, stride=4), :] = disp_ref[c]
        first = below_ref[5:6, c * nodes : (c + 1) * nodes]
        prior[c : c + 1, :] = jnp.where(keep_ref[0] > 0, first, 0.0)
    here[pl.ds(3, count, stride=4), :] = jnp.zeros((count, nodes), f32)
    prior[pl.ds(3, count + 1, stride=4), :] = jnp.zeros((count + 1, nodes), f32)
    for copy in copies:
        copy.wait()
    for k in range(count // 2):
        rows = slice(8 * k, 8 * k + 8)
        left = jnp.concatenate([here[rows, :], prior[rows, :]], axis=1).astype(bf16)
        right = jnp.concatenate(
            [
                jnp.concatenate([stiff_ref[2 * k], stiff_ref[2 * k + 1]], axis=0),
                jnp.concatenate([coup_ref[2 * k], coup_ref[2 * k + 1]], axis=0),
            ],
            axis=1,
        )
        made[rows, :] = pick_half(nt_dot(left, right))
    for c in range(3):
        out_ref[c] = made[pl.ds(c, count, stride=4), :]


def residual(got_ref, kd_ref, inv_ref, disp_ref, diff_ref, base_ref, share_ref):
    count, nodes = disp_ref.shape[1:]
    peers = share_ref.shape[0]
    turned = got_ref[pl.ds(sent_rows - 1, peers, stride=sent_rows), :].T
    block = iota((count, peers), 0).astype(f32)
    chosen = jnp.concatenate(
        [jnp.where(block == turned[i : i + 1, :], 1.0, 0.0) for i in range(2)], axis=1
    ).astype(bf16)
    res = []
    for c in range(3):
        rows = jnp.concatenate(
            [got_ref[pl.ds(c + 3 * i, peers, stride=sent_rows), :] for i in range(2)], axis=0
        )
        part = -inv_ref[c] * (kd_ref[c] - exact_dot(chosen, rows))
        base_ref[c] = disp_ref[c] + part
        res.append(part)
    columns = diff_ref.shape[0]
    sums = []
    for m in range(columns):
        part = sum(diff_ref[m, c] * res[c] for c in range(3))
        sums.append(jnp.sum(part, axis=0, keepdims=True))
    col = jnp.sum(jnp.concatenate(sums, axis=0), axis=1, keepdims=True)
    diag = iota((columns, nodes), 0) == iota((columns, nodes), 1)
    row = jnp.sum(jnp.where(diag, col, 0.0), axis=0, keepdims=True)
    share_ref[...] = jnp.broadcast_to(row, share_ref.shape)


def factor(
    blocks, got_ref, dd_hbm, inverse_ref, serve_ref, turned_ref, dd_ref, semaphores, spread
):
    copies = fetch((dd_hbm,), (dd_ref,), semaphores)
    lanes = serve_ref.shape[1]
    peers = serve_ref.shape[0] // reply_rows
    meta = got_ref[pl.ds(sent_rows - 1, peers, stride=sent_rows), :]
    block = iota((peers, lanes), 1).astype(f32)
    for i in range(2):
        tag = jnp.broadcast_to(meta[:, i : i + 1], (peers, lanes))
        for c in range(3):
            wanted = jnp.where(tag >= 0.0, tag + float(c * blocks), -1.0)
            hot = jnp.where(block == wanted, 1.0, 0.0)
            spread[pl.ds(2 * c + i, peers, stride=reply_rows), :] = hot
    serve_ref[...] = spread[...].astype(bf16)
    row = iota((8, lanes), 0)
    lane = iota((8, lanes), 1)
    total = jnp.sum(meta, axis=0, keepdims=True)
    total = pltpu.roll(total, lanes - gram_lane, 1)
    n = 8
    gram = jnp.concatenate(
        [total if m == 0 else pltpu.roll(total, lanes - n * m, 1) for m in range(n)], axis=0
    )
    work = jnp.where(lane < n, gram, jnp.where(lane == row + n, 1.0, 0.0))
    for k in range(n):
        pivot = work[k : k + 1, :] * lax.rsqrt(work[k : k + 1, k : k + 1])
        below = work[:, k : k + 1] * lax.rsqrt(work[k : k + 1, k : k + 1])
        work = jnp.where(row == k, pivot, jnp.where(row > k, work - below * pivot, work))
    inverse = jnp.where(lane < n, pltpu.roll(work, lanes - n, 1), 0.0)
    inverse_ref[...] = inverse
    copies[0].wait()
    for k in range(n):
        for c in range(3):
            turned_ref[k, c] = sum(
                inverse[k : k + 1, m : m + 1] * dd_ref[m, c] for m in range(k + 1)
            )


def update(share_ref, inverse_ref, base_ref, turned_ref, serve_ref, next_ref, reply_ref):
    projected = jnp.sum(share_ref[...], axis=0, keepdims=True)
    middle = jnp.sum(inverse_ref[...] * projected, axis=1, keepdims=True)
    rows = []
    for c in range(3):
        value = base_ref[c]
        for k in range(turned_ref.shape[0]):
            value = value - middle[k : k + 1, :] * turned_ref[k, c]
        next_ref[c] = value
        rows.append(value)
    blocks = jnp.concatenate(rows, axis=0).astype(bf16)
    spare = serve_ref.shape[1] - blocks.shape[0]
    blocks = jnp.concatenate([blocks, jnp.zeros((spare, blocks.shape[1]), bf16)], axis=0)
    reply_ref[...] = jnp.dot(
        serve_ref[...], blocks, preferred_element_type=f32
    ).astype(bf16)


def prepare(slot_ref, rbf_hbm, pick_ref, turned_ref, rbf_ref, semaphores):
    copies = fetch((rbf_hbm,), (rbf_ref,), semaphores)
    wanted = iota(pick_ref.shape, 1).astype(f32) == slot_ref[...]
    pick_ref[...] = jnp.where(wanted, 1.0, 0.0).astype(bf16)
    copies[0].wait()
    for b in range(rbf_ref.shape[0]):
        turned_ref[b] = rbf_ref[b].T


def motion(back_ref, pick_ref, turned_ref, out_ref, picked, made):
    count = turned_ref.shape[0]
    picked[...] = jnp.dot(pick_ref[...], back_ref[...], preferred_element_type=f32)
    for k in range(count // 2):
        rows = slice(8 * k, 8 * k + 8)
        both = jnp.concatenate([turned_ref[2 * k], turned_ref[2 * k + 1]], axis=1)
        left = picked[rows, :].astype(bf16)
        made[rows, :] = pick_half(jnp.dot(left, both, preferred_element_type=f32))
    for c in range(3):
        out_ref[c] = made[pl.ds(c, count, stride=4), :]


def exchange(value):
    return lax.all_to_all(value, AXES[::-1], split_axis=0, concat_axis=0, tiled=True)


def on_device(
    density, velocity, pressure, rbf, correlation, normals, routes, targets,
    stiffness, coupling, inverse_diag, displacement, diff_res, diff_disp,
):
    peers = lax.axis_size(AXES)
    depth, lanes = density.shape[1:]
    wide = -(-depth // 128) * 128
    count, nodes = correlation.shape
    blocks = displacement.shape[0]
    columns = diff_res.shape[0]
    normals, inverse_diag, displacement = (
        jnp.transpose(x, (1, 0, 2)) for x in (normals, inverse_diag, displacement)
    )
    diff_res, diff_disp = (jnp.transpose(x, (0, 2, 1, 3)) for x in (diff_res, diff_disp))
    ring = [(i, (i + 1) % peers) for i in range(peers)]
    back = [(j, i) for i, j in ring]

    own, second = call(
        edges,
        [shape((8, wide)), shape((8, wide))],
        density, velocity, pressure, displacement,
        fetched=(0, 1, 2, 3),
    )
    above = lax.ppermute(own, AXES, back)
    below = lax.ppermute(own, AXES, ring)
    kernel = functools.partial(routing, lax.axis_size(AXES[0]))
    kernel.__name__ = "routing"
    start, scatter, slot, meta, bulk, corr_near, normals_near, rbf_near = call(
        kernel,
        [
            shape((8, wide)),
            shape((sent_rows * peers, 4 * count), bf16),
            shape((4 * count, 1)),
            shape((peers, nodes)),
            shape((5, depth, lanes), bf16),
            shape(correlation.shape, jnp.int32),
            shape(normals.shape),
            shape(rbf.shape, bf16),
        ],
        routes.reshape(1, count), targets.reshape(1, count), diff_res,
        density, velocity, pressure, correlation, normals, rbf, own, second,
        fetched=(0, 1, 2, 3, 4, 5),
        remote=(6, 7, 8),
        scratch=[pltpu.SemaphoreType.DMA((3,))],
    )
    bulk_below = lax.ppermute(bulk, AXES, ring)
    bulk_above = lax.ppermute(bulk, AXES, back)
    keep = (lax.axis_index(AXES) > 0).astype(jnp.int32).reshape(1)
    product = call(
        solid,
        shape((3, blocks, nodes)),
        keep, displacement, below, stiffness, coupling,
        fetched=(3, 4),
        scalars=(0,),
        scratch=[
            pltpu.VMEM((4 * blocks, nodes), f32),
            pltpu.VMEM((4 * blocks + 8, nodes), f32),
            pltpu.VMEM((4 * blocks, nodes), f32),
        ],
    )
    sent = call(
        loads,
        shape((sent_rows * peers, nodes)),
        start, own, below, above, corr_near, normals_near, rbf_near, scatter, meta, product,
        scratch=[pltpu.VMEM((4 * count, nodes), f32)] * 2,
    )
    got = exchange(sent.reshape(peers, 1, sent_rows * nodes)).reshape(sent_rows * peers, nodes)
    base, share = call(
        residual,
        [shape((3, blocks, nodes)), shape((peers, nodes))],
        got, product, inverse_diag, displacement, diff_res,
    )
    shares = exchange(share)
    kernel = functools.partial(factor, blocks)
    kernel.__name__ = "factor"
    inverse, serve, turned = call(
        kernel,
        [
            shape((columns, nodes)),
            shape((reply_rows * peers, nodes), bf16),
            shape((columns, 3, blocks, nodes)),
        ],
        got, diff_disp,
        fetched=(1,),
        scratch=[pltpu.VMEM((reply_rows * peers, nodes), f32)],
    )
    disp_next, reply = call(
        update,
        [shape((3, blocks, nodes)), shape((reply_rows * peers, nodes), bf16)],
        shares, inverse, base, turned, serve,
    )
    reply = jnp.transpose(reply.reshape(peers, 3, 2, nodes), (0, 2, 1, 3))
    returned = exchange(reply.reshape(peers, 2, 3 * nodes)).reshape(peers, 2, 3, nodes)
    returned = jnp.transpose(returned, (0, 2, 1, 3)).reshape(reply_rows * peers, nodes)
    fluid_next = call(
        fluid,
        shape((5, 1, depth, lanes)),
        density, velocity, pressure, bulk_below, bulk_above,
        fetched=(0, 1, 2, 3, 4),
    )
    pick, rbf_turned = call(
        prepare,
        [shape((4 * count, reply_rows * peers), bf16), shape(rbf.shape, bf16)],
        slot, rbf,
        fetched=(1,),
    )
    wall_motion = call(
        motion,
        shape((3, count, nodes)),
        returned, pick, rbf_turned,
        scratch=[pltpu.VMEM((4 * count, nodes), f32)] * 2,
    )
    return (
        fluid_next,
        jnp.transpose(disp_next, (1, 0, 2)),
        jnp.transpose(wall_motion, (1, 0, 2)),
    )


def solution(mesh):
    rows = P(AXES, None, None)
    inner = P(None, AXES, None, None)
    return jax.shard_map(
        on_device,
        mesh=mesh,
        in_specs=(
            rows, inner, rows, rows, P(AXES, None), rows, P(AXES, None), P(AXES),
            rows, rows, rows, rows, inner, inner,
        ),
        out_specs=(inner, rows, rows),
        check_vma=False,
    )
```
